32 devices in a mesh: pipe: 2 (over x), dp: 4 (over z), expert: 4 (over y, core).
Axes of the slice: x: 2, y: 2, z: 4, core: 2. Of those that a mesh axis runs over, the one named last changes fastest.
Arguments:
- out_grad: bfloat16 [2, 2, 512, 3072], P('pipe', None, 'expert', 'dp'), may hold values from -6 to 6
- expert_outputs: bfloat16 [2, 2, 512, 2, 3072], P('pipe', None, 'expert', None, 'dp'), may hold values from -0.1796875 to 0.1796875
- logits: float32 [2, 2, 512, 2], P('pipe', None, 'expert'), may hold values from -9 to 9
- routes: int32 [2, 2, 512, 2], P('pipe', None, 'expert'), may hold values from 0 to 3, all different within a row; in each aligned block of 128 rows (0 to 127, 128 to 255, ..., all dimensions but the last counted through in order) at most 68 rows name the same one
- down_weights: bfloat16 [4, 16384, 3072], P('expert', 'dp'), may hold values from -0.046875 to 0.046875
Outputs:
- grad_hidden: bfloat16 [2, 2, 4, 4, 68, 16384], P('pipe', None, 'expert', None, None, 'dp')
- grad_logits: bfloat16 [2, 2, 512, 2], P('pipe', None, 'expert')
The draws below stay inside these ranges and needn't reach their ends.
Inputs may be any that keep to these rules, and one draw needn't show every extreme that they name: `routes`: each token names two different experts. The 128 tokens of one group, section and micro-batch (aligned blocks of 128 tokens) name one expert at most 68 times, and in every draw some block names some expert exactly 68 times.
All inputs are finite; a program needn't handle non-finite values.
Results may differ from the reference program's by a relative error of at most 0.0049.
Values may be sent and summed in bfloat16 or wider, within the bound.
No kernel may reach another device: no remote copies, remote signals or barrier semaphores. Data moves between devices by JAX's collectives and lax.ppermute only.
A program may use at most 64 MiB of HBM per device.

```python
import math
import jax
import jax.numpy as jnp
import numpy as np
from jax import lax

D = 3072
FF = 16384
TOK_DEV = 128
MICRO = 2
EXPERTS = 4
GROUPS = 4
SECTIONS = 2
TOKENS = 512
CAP = 68


def steps_of(own_key, shape, shards, least, high):
    level, own = 1.0, jax.random.fold_in(own_key, 6)
    for dim, blocks in shards:
        heights = jnp.exp(jax.random.uniform(jax.random.fold_in(own, dim), (blocks,), jnp.float32, least / len(shards), high / len(shards)))
        level = level * jnp.repeat(heights, shape[dim] // blocks).reshape([-1 if axis == dim else 1 for axis in range(len(shape))])
    return level


def assign_block(stream_key, own, number, rows, amount, top, limit, lean):
    order = jax.random.permutation(stream_key, amount)
    heavy_load, common = load_shares(amount, rows * top, limit, lean, True), load_shares(amount, rows * top, limit, lean, False)
    places = jnp.arange(amount)

    def named(tallies, turn):
        used = int((tallies > 0).sum())
        fixed = max(1, used // 4)
        passed = fixed + (places - fixed + turn * (used - fixed)) % max(1, amount - fixed)
        return jnp.zeros((amount,), jnp.int32).at[order[jnp.where(places < fixed, places, passed)]].set(jnp.asarray(tallies, jnp.int32))

    tallies = jnp.where(number % 4 == 0, named(heavy_load, number // 4), named(common, number - number // 4 - 1))
    mixed = jax.random.permutation(jax.random.fold_in(own, 3), amount)
    donor, taker = mixed[0:amount // 2 * 2:2], mixed[1:amount // 2 * 2:2]
    room = jnp.minimum(tallies[donor] - 1, limit - tallies[taker]) // 2
    room = jnp.where((donor == order[0]) | (taker == order[0]) | (tallies[taker] == 0), 0, jnp.maximum(room, 0))
    passed = jax.random.randint(jax.random.fold_in(own, 4), (amount // 2,), 0, 1 << 20) % (room + 1)
    tallies = tallies.at[donor].add(-passed).at[taker].add(passed)
    members = jnp.searchsorted(jnp.cumsum(tallies), jnp.arange(rows * top), side="right").astype(jnp.int32)
    table = members.reshape(top, rows).T
    table = table[jax.random.permutation(jax.random.fold_in(own, 1), rows)]
    turn = jax.random.randint(jax.random.fold_in(own, 2), (rows, 1), 0, top)
    return jnp.take_along_axis(table, (jnp.arange(top)[None, :] + turn) % top, axis=1)


def load_shares(number_of, total, most, skew, full):
    portions = [(1 << 20) // math.isqrt(grade ** skew) + 1 for grade in range(1, number_of + 1)]
    largest = most if full else min(most, max(-(-total // number_of), total * portions[0] // sum(portions)))
    least = 1 if total - largest >= number_of - 1 else 0
    given, surplus = [largest] + [least] * (number_of - 1), total - largest - least * (number_of - 1)
    while surplus > 0:
        candidates = [i for i in range(1, number_of) if given[i] < largest] or [i for i in range(1, number_of) if given[i] < most]
        mass, budget = sum([portions[i] for i in candidates]), surplus
        for i in candidates:
            more = min(most - given[i], max(1, budget * portions[i] // mass), surplus)
            given[i] = given[i] + more
            surplus = surplus - more
    return np.array(given)


def bell_draw(own_key, shape, spread, limit, shards=(), held_as=jnp.bfloat16):
    level = steps_of(own_key, shape, shards, -0.22, 0.18) if shards else 1.0
    values = jax.random.normal(own_key, shape, jnp.float32) * spread * level
    return jnp.minimum(jnp.maximum(values, -limit), limit).astype(held_as)


def setup_inputs(seed: int = 0) -> dict:
    key_of = jax.random.split(jax.random.key(seed), 6)
    out_grad = bell_draw(key_of[0], (SECTIONS, MICRO, TOKENS, D), 1.0, 6.0, ((0, 2), (2, 4), (3, 4)))
    expert_outputs = bell_draw(key_of[1], (SECTIONS, MICRO, TOKENS, 2, D), 0.03, 0.1796875, ((0, 2), (2, 4), (4, 4)))
    logits = bell_draw(key_of[2], (SECTIONS, MICRO, TOKENS, 2), 1.5, 9.0, ((0, 2), (2, 4)), jnp.float32)
    routes_keys = jax.random.split(jax.random.fold_in(key_of[3], 1), SECTIONS * MICRO * TOKENS // TOK_DEV)
    routes_turns = jax.random.permutation(jax.random.fold_in(key_of[3], 3), SECTIONS * MICRO * TOKENS // TOK_DEV)
    routes = jax.vmap(lambda own, number: assign_block(jax.random.fold_in(key_of[3], 2), own, number, TOK_DEV, EXPERTS, 2, CAP, 1))(routes_keys, routes_turns).reshape((SECTIONS, MICRO, TOKENS, 2))
    down_weights = bell_draw(key_of[4], (EXPERTS, FF, D), FF ** -0.5, 0.046875, ((0, 4), (1, 4)))
    return dict(out_grad=out_grad, expert_outputs=expert_outputs, logits=logits, routes=routes, down_weights=down_weights)


def section_terms(out_grad, expert_outputs, logits, routes, weights):
    weight_first = jax.nn.sigmoid(logits[..., 0] - logits[..., 1])
    weight_second = jax.nn.sigmoid(logits[..., 1] - logits[..., 0])
    scores = jnp.einsum('mtkd,mtd->mtk', expert_outputs.astype(jnp.float32), out_grad.astype(jnp.float32))
    difference = weight_first * weight_second * (scores[..., 0] - scores[..., 1])
    logit_grad = jnp.stack([difference, -difference], -1)
    pair_weights = jnp.stack([weight_first, weight_second], -1)
    pair_routes = routes.reshape(MICRO, GROUPS, 2 * TOK_DEV)
    onehot = (pair_routes[..., None] == jnp.arange(EXPERTS, dtype=jnp.int32)).astype(jnp.int32)
    earlier = jnp.cumsum(onehot, axis=2) - onehot
    slot_index = jnp.sum(earlier * onehot, -1)
    target_slot = pair_routes * CAP + slot_index
    placement = (target_slot[..., None] == jnp.arange(EXPERTS * CAP, dtype=jnp.int32)).astype(jnp.float32)
    weighted_rows = (pair_weights[..., None] * out_grad[:, :, None, :].astype(jnp.float32)).astype(jnp.bfloat16)
    weighted_rows = weighted_rows.reshape(MICRO, GROUPS, 2 * TOK_DEV, D)
    dispatched = jnp.einsum('mgpq,mgpd->mgqd', placement, weighted_rows.astype(jnp.float32)).astype(jnp.bfloat16)
    dispatched = dispatched.reshape(MICRO, GROUPS, EXPERTS, CAP, D).transpose(0, 2, 1, 3, 4)
    hidden_grad = jnp.einsum('megcd,efd->megcf', dispatched.astype(jnp.float32), weights)
    return hidden_grad.astype(jnp.bfloat16), logit_grad.astype(jnp.bfloat16)


def reference(out_grad, expert_outputs, logits, routes, down_weights):
    weights = down_weights.astype(jnp.float32)

    def one_section(items):
        return section_terms(items[0], items[1], items[2], items[3], weights)

    hidden_all, logit_all = lax.map(one_section, (out_grad, expert_outputs, logits, routes))
    grad_hidden = jnp.concatenate([hidden_all[1:], jnp.zeros_like(hidden_all[:1])], 0)
    grad_logits = jnp.concatenate([logit_all[1:], jnp.zeros_like(logit_all[:1])], 0)
    return grad_hidden, grad_logits
```

```python
import functools

import jax
import jax.numpy as jnp
from jax import lax
from jax.experimental import pallas as pl
from jax.experimental.pallas import tpu as pltpu
from jax.sharding import PartitionSpec as P

MEBI = 1024 * 1024
NT = (((1,), (1,)), ((), ()))


def hop(x, pipe_by, dp_xor):
    sections, shares = lax.axis_size("pipe"), lax.axis_size("dp")
    pairs = [
        (s * shares + z, (s - pipe_by) * shares + (z ^ dp_xor))
        for s in range(pipe_by, sections)
        for z in range(shares)
    ]
    return lax.ppermute(x, ("pipe", "dp"), pairs)


def swap(x, bit):
    sections, experts = lax.axis_size("pipe"), lax.axis_size("expert")
    pairs = [
        (s * experts + e, s * experts + (e ^ bit))
        for s in range(sections - 1)
        for e in range(experts)
    ]
    return lax.ppermute(x, ("pipe", "expert"), pairs)


def spread(x):
    bit = lax.axis_size("expert") // 2
    held = {0: x}
    while bit:
        for j in sorted(held):
            held[j ^ bit] = swap(held[j], bit)
        bit //= 2
    return [held[j] for j in sorted(held)]


def fill_rows(place_ref, meta_ref, token_refs, rows_ref, cap, padded):
    expert = place_ref[0].astype(jnp.float32)
    groups = len(token_refs)
    tokens = meta_ref.shape[2]
    micros = meta_ref.shape[1] // 4
    earlier = lax.broadcasted_iota(jnp.int32, (tokens, tokens), 0) < lax.broadcasted_iota(
        jnp.int32, (tokens, tokens), 1
    )
    earlier = earlier.astype(jnp.bfloat16)
    slots = lax.broadcasted_iota(jnp.int32, (padded, tokens), 0).astype(jnp.float32)
    for micro in range(micros):
        blocks = []
        for j in range(groups):
            meta = meta_ref[j]
            first = meta[4 * micro : 4 * micro + 1] == expert
            second = meta[4 * micro + 1 : 4 * micro + 2] == expert
            here = jnp.logical_or(first, second)
            weight = jnp.where(
                first, meta[4 * micro + 2 : 4 * micro + 3], meta[4 * micro + 3 : 4 * micro + 4]
            )
            named = jnp.broadcast_to(here.astype(jnp.float32), (16, tokens)).astype(jnp.bfloat16)
            slot = jnp.dot(named, earlier, preferred_element_type=jnp.float32)[0:1]
            picked = jnp.logical_and(slots == slot, here)
            picked = jnp.logical_and(picked, slots < cap)
            row_weight = jnp.sum(jnp.where(picked, weight, 0.0), axis=1, keepdims=True)
            block = jnp.dot(
                picked.astype(jnp.float32).astype(jnp.bfloat16),
                token_refs[j][micro * tokens : (micro + 1) * tokens, :],
                preferred_element_type=jnp.float32,
            )
            blocks.append(block * row_weight)
        for j in range(0, groups, 2):
            at = (micro * groups + j) * padded
            rows_ref[at : at + 2 * padded, :] = jnp.concatenate(blocks[j : j + 2], 0).astype(
                jnp.bfloat16
            )


def part_kernel(groups, cap, padded, first, last, *refs):
    place_ref, meta_ref = refs[:2]
    token_refs = refs[2 : 2 + groups]
    weight_ref = refs[2 + groups]
    rest = refs[3 + groups :]
    total_ref = None
    if not first:
        total_ref, rest = rest[0], rest[1:]
    out_ref, rows_ref = rest

    @pl.when(pl.program_id(0) == 0)
    def _():
        fill_rows(place_ref, meta_ref, token_refs, rows_ref, cap, padded)

    product = lax.dot_general(
        rows_ref[...], weight_ref[0], NT, preferred_element_type=jnp.float32
    )
    if not first:
        product = product + total_ref[...]
    if not last:
        out_ref[...] = product
    else:
        for micro in range(out_ref.shape[1]):
            for j in range(groups):
                at = (micro * groups + j) * padded
                out_ref[0, micro, 0, place_ref[0] ^ j] = product[at : at + cap].astype(
                    out_ref.dtype
                )


def add_part(place, meta, tokens, weights, total, cap, last):
    groups = len(tokens)
    micros = meta.shape[1] // 4
    padded = -(-cap // 8) * 8
    rows = micros * groups * padded
    depth = tokens[0].shape[1]
    hidden = weights.shape[1]
    block = min(512, hidden)
    whole = lambda *shape: pl.BlockSpec(shape, lambda f, p: (0,) * len(shape))
    in_specs = [whole(*meta.shape)] + [whole(*t.shape) for t in tokens]
    in_specs.append(pl.BlockSpec((1, block, depth), lambda f, p: (0, f, p[1])))
    args = [place, meta, *tokens, weights]
    aliases = {}
    total_spec = pl.BlockSpec((rows, block), lambda f, p: (0, f))
    if total is not None:
        in_specs.append(total_spec)
        args.append(total)
        if not last:
            aliases = {len(args) - 1: 0}
    if last:
        out_shape = jax.ShapeDtypeStruct((1, micros, 1, groups, cap, hidden), jnp.bfloat16)
        out_spec = pl.BlockSpec(
            (1, micros, 1, groups, cap, block), lambda f, p: (0, 0, 0, 0, 0, f)
        )
    else:
        out_shape = jax.ShapeDtypeStruct((rows, hidden), jnp.float32)
        out_spec = total_spec
    return pl.pallas_call(
        functools.partial(part_kernel, groups, cap, padded, total is None, last),
        grid_spec=pltpu.PrefetchScalarGridSpec(
            num_scalar_prefetch=1,
            grid=(hidden // block,),
            in_specs=in_specs,
            out_specs=out_spec,
            scratch_shapes=[pltpu.VMEM((rows, depth), jnp.bfloat16)],
        ),
        out_shape=out_shape,
        input_output_aliases=aliases,
        compiler_params=pltpu.CompilerParams(vmem_limit_bytes=40 * MEBI),
        cost_estimate=pl.CostEstimate(
            flops=2 * rows * depth * hidden,
            bytes_accessed=2 * hidden * depth + 8 * rows * hidden,
            transcendentals=0,
        ),
    )(*args)


def per_device(out_grad, expert_outputs, logits, routes, down_weights):
    micros, token_count, share = out_grad.shape[1:]
    experts, shares = lax.axis_size("expert"), lax.axis_size("dp")
    cap = min(token_count, 2 * token_count // experts + token_count // 32)
    expert, mine = lax.axis_index("expert"), lax.axis_index("dp")

    own = out_grad.reshape(micros * token_count, share)
    together = 1
    while (share * together) % 128:
        together *= 2
    arrived = [hop(own, 1, k) for k in range(shares)]

    grads = out_grad[0].astype(jnp.float32)
    outputs = expert_outputs[0].astype(jnp.float32)
    difference = jnp.sum(grads * (outputs[:, :, 0] - outputs[:, :, 1]), -1)
    weight_first = jax.nn.sigmoid(logits[0, ..., 0] - logits[0, ..., 1])
    weight_second = jax.nn.sigmoid(logits[0, ..., 1] - logits[0, ..., 0])
    named = routes[0].astype(jnp.float32)
    meta = jnp.stack([named[..., 0], named[..., 1], weight_first, weight_second], 1)
    meta = meta.reshape(4 * micros, token_count)
    small = jnp.concatenate([meta, difference], 0)
    smalls = [hop(small, 1, k) for k in range(shares)]
    meta = smalls[0][: 4 * micros]
    score = sum(s[4 * micros :] for s in smalls)
    by_micro = meta.reshape(micros, 4, token_count)
    slope = by_micro[:, 2] * by_micro[:, 3] * score
    moved_logits = jnp.stack([slope, -slope], -1).astype(jnp.bfloat16)[None]

    metas = jnp.stack(spread(meta))
    total = None
    for part in range(0, shares, together):
        pieces = [spread(arrived[part + i]) for i in range(together)]
        low = mine % together
        tokens = []
        for j in range(experts):
            if together == 1:
                tokens.append(pieces[0][j])
            else:
                stacked = jnp.stack([piece[j] for piece in pieces])
                order = jnp.arange(together) ^ low
                tokens.append(
                    jnp.take(stacked, order, axis=0).transpose(1, 0, 2).reshape(
                        micros * token_count, together * share
                    )
                )
        place = jnp.stack([expert, (mine ^ part) // together]).astype(jnp.int32)
        total = add_part(
            place, metas, tokens, down_weights, total, cap, part + together == shares
        )
    return total, moved_logits


def solution(mesh):
    in_specs = (
        P("pipe", None, "expert", "dp"),
        P("pipe", None, "expert", None, "dp"),
        P("pipe", None, "expert", None),
        P("pipe", None, "expert", None),
        P("expert", "dp", None),
    )
    out_specs = (P("pipe", None, "expert", None, None, "dp"), P("pipe", None, "expert", None))
    return jax.shard_map(
        per_device, mesh=mesh, in_specs=in_specs, out_specs=out_specs, check_vma=False
    )
```

```python
import functools

import jax
import jax.numpy as jnp
from jax import lax
from jax.experimental import pallas as pl
from jax.experimental.pallas import tpu as pltpu
from jax.sharding import PartitionSpec as P

MEBI = 1024 * 1024
NT = (((1,), (1,)), ((), ()))
EXTRA = 16


def from_next(x):
    sections = lax.axis_size("pipe")
    return lax.ppermute(x, "pipe", [(s, (s - 1) % sections) for s in range(sections)])


def from_next_share(x, dp_xor):
    sections, shares = lax.axis_size("pipe"), lax.axis_size("dp")
    pairs = [
        (s * shares + z, (s - 1) * shares + (z ^ dp_xor))
        for s in range(1, sections)
        for z in range(shares)
    ]
    return lax.ppermute(x, ("pipe", "dp"), pairs)


def from_share(x, dp_xor):
    sections, shares = lax.axis_size("pipe"), lax.axis_size("dp")
    pairs = [
        (s * shares + z, s * shares + (z ^ dp_xor))
        for s in range(sections - 1)
        for z in range(shares)
    ]
    return lax.ppermute(x, ("pipe", "dp"), pairs)


def swap(x, bit):
    experts = lax.axis_size("expert")
    return lax.ppermute(x, "expert", [(e, e ^ bit) for e in range(experts)])


def after(x, *first):
    return lax.optimization_barrier((x, *first))[0]


def thirds(x):
    high = lax.reduce_precision(x, 8, 7)
    middle = lax.reduce_precision(x - high, 8, 7)
    return [high, middle, x - high - middle]


def place_kernel(expert_ref, meta_ref, places_ref, weights_ref):
    expert = expert_ref[0]
    groups, _, tokens = meta_ref.shape
    micros = meta_ref.shape[1] // 4
    rows = places_ref.shape[1]
    earlier = lax.broadcasted_iota(jnp.int32, (tokens, tokens), 0) < lax.broadcasted_iota(
        jnp.int32, (tokens, tokens), 1
    )
    earlier = earlier.astype(jnp.bfloat16)
    row = lax.broadcasted_iota(jnp.int32, (rows, tokens), 0)
    weights = []
    for micro in range(micros):
        for j in range(groups):
            meta = meta_ref[j]
            first = meta[4 * micro : 4 * micro + 1] == expert.astype(jnp.float32)
            second = meta[4 * micro + 1 : 4 * micro + 2] == expert.astype(jnp.float32)
            here = jnp.logical_or(first, second)
            weights.append(
                jnp.where(
                    first, meta[4 * micro + 2 : 4 * micro + 3], meta[4 * micro + 3 : 4 * micro + 4]
                )
            )
            named = jnp.broadcast_to(here.astype(jnp.float32), (16, tokens)).astype(jnp.bfloat16)
            slot = jnp.dot(named, earlier, preferred_element_type=jnp.float32)[0:1]
            target = slot.astype(jnp.int32) * groups + (expert ^ j)
            picked = row == jnp.where(here, target, -1)
            places_ref[micro, :, j * tokens : (j + 1) * tokens] = picked.astype(
                jnp.float32
            ).astype(jnp.bfloat16)
    weights = jnp.concatenate(weights, 0)
    padding = jnp.zeros((tokens - weights.shape[0], tokens), jnp.float32)
    weights_ref[...] = jnp.transpose(jnp.concatenate([weights, padding], 0))


def find_places(expert, meta, cap):
    groups, quads, tokens = meta.shape
    micros = quads // 4
    in_vmem = pl.BlockSpec(memory_space=pltpu.VMEM)
    return pl.pallas_call(
        place_kernel,
        in_specs=[pl.BlockSpec(memory_space=pltpu.SMEM), in_vmem],
        out_specs=[in_vmem, in_vmem],
        out_shape=[
            jax.ShapeDtypeStruct((micros, cap * groups, groups * tokens), jnp.bfloat16),
            jax.ShapeDtypeStruct((tokens, tokens), jnp.float32),
        ],
        compiler_params=pltpu.CompilerParams(vmem_limit_bytes=16 * MEBI),
    )(expert, meta)


def fill_kernel(cut, places_ref, weights_ref, *refs):
    token_refs, rows_ref = refs[:-1], refs[-1]
    micros, rows, _ = places_ref.shape
    tokens = weights_ref.shape[0]
    half = len(token_refs)
    late = micros * tokens - cut
    for micro in range(micros):
        blocks = []
        for j in range(2 * half):
            source, top = token_refs[j % half], j // half
            low, high = micro * tokens, (micro + 1) * tokens
            pieces = []
            if low < cut:
                pieces.append(source[top * cut + low : top * cut + min(high, cut), :])
            if high > cut:
                at = 2 * cut + top * late - cut
                pieces.append(source[at + max(low, cut) : at + high, :])
            held = pieces[0] if len(pieces) == 1 else jnp.concatenate(pieces, 0)
            weight = weights_ref[:, micro * 2 * half + j : micro * 2 * half + j + 1]
            blocks.append((held.astype(jnp.float32) * weight).astype(jnp.bfloat16))
        rows_ref[micro * rows : (micro + 1) * rows, :] = jnp.dot(
            places_ref[micro], jnp.concatenate(blocks, 0), preferred_element_type=jnp.float32
        ).astype(jnp.bfloat16)


def fill_rows(places, weights, tokens, cut):
    micros, rows, _ = places.shape
    depth = tokens[0].shape[1]
    in_vmem = pl.BlockSpec(memory_space=pltpu.VMEM)
    return pl.pallas_call(
        functools.partial(fill_kernel, cut),
        in_specs=[in_vmem] * (2 + len(tokens)),
        out_specs=in_vmem,
        out_shape=jax.ShapeDtypeStruct((micros * rows, depth), jnp.bfloat16),
        compiler_params=pltpu.CompilerParams(vmem_limit_bytes=24 * MEBI),
    )(places, weights, *tokens)


def part_kernel(parts, groups, first, last, *refs):
    place_ref = refs[0]
    row_refs = refs[1 : 1 + parts]
    weight_ref = refs[1 + parts]
    rest = refs[2 + parts :]
    step = pl.program_id(0)
    block, depth = weight_ref.shape[1], row_refs[0].shape[1]
    here = pl.ds(pl.multiple_of(step * block, block), block)
    product = None
    for part in range(parts):
        at = pl.multiple_of((place_ref[1] ^ part) * depth, depth)
        term = lax.dot_general(
            row_refs[part][...],
            weight_ref[0, :, pl.ds(at, depth)],
            NT,
            preferred_element_type=jnp.float32,
        )
        product = term if product is None else product + term
    if not first:
        product = product + rest[0][:, here]
    out_ref = rest[-1]
    if not last:
        out_ref[:, here] = product
    else:
        micros, cap = out_ref.shape[1], out_ref.shape[3]
        rows = cap * groups
        for micro in range(micros):
            out_ref[0, micro, 0] = (
                product[micro * rows : (micro + 1) * rows]
                .reshape(cap, groups, block)
                .astype(out_ref.dtype)
            )


def add_part(place, rows, weights, total, micros, groups, last):
    count, depth = rows[0].shape
    hidden = weights.shape[1]
    block = min(1024, hidden)
    in_vmem = pl.BlockSpec(memory_space=pltpu.VMEM)
    in_specs = [in_vmem] * len(rows)
    in_specs.append(pl.BlockSpec((1, block, depth * len(rows)), lambda f, p: (0, f, p[0])))
    args = [place, *rows, weights]
    if total is not None:
        in_specs.append(in_vmem)
        args.append(total)
    if last:
        cap = count // (micros * groups)
        out_shape = jax.ShapeDtypeStruct((1, micros, 1, cap, groups, hidden), jnp.bfloat16)
        out_spec = pl.BlockSpec(
            (1, micros, 1, cap, groups, block), lambda f, p: (0, 0, 0, 0, 0, f)
        )
    else:
        out_shape = jax.ShapeDtypeStruct((count, hidden), jnp.float32)
        out_spec = in_vmem
    return pl.pallas_call(
        functools.partial(part_kernel, len(rows), groups, total is None, last),
        grid_spec=pltpu.PrefetchScalarGridSpec(
            num_scalar_prefetch=1,
            grid=(hidden // block,),
            in_specs=in_specs,
            out_specs=out_spec,
        ),
        out_shape=out_shape,
        compiler_params=pltpu.CompilerParams(vmem_limit_bytes=36 * MEBI),
        cost_estimate=pl.CostEstimate(
            flops=2 * count * depth * len(rows) * hidden,
            bytes_accessed=2 * hidden * depth * len(rows),
            transcendentals=0,
        ),
    )(*args)


def per_device(out_grad, expert_outputs, logits, routes, down_weights):
    micros, token_count, share = out_grad.shape[1:]
    experts, shares = lax.axis_size("expert"), lax.axis_size("dp")
    cap = min(token_count, 2 * token_count // experts + token_count // 32)
    expert, mine = lax.axis_index("expert"), lax.axis_index("dp")
    received = lax.axis_index("pipe") < lax.axis_size("pipe") - 1
    top = experts // 2

    own = out_grad.reshape(micros * token_count, share)
    cut = micros * token_count * 11 // 16
    early, late = own[:cut], own[cut:]

    grads = out_grad[0].astype(jnp.float32)
    outputs = expert_outputs[0].astype(jnp.float32)
    difference = jnp.sum(grads * (outputs[:, :, 0] - outputs[:, :, 1]), -1)
    named = routes[0].astype(jnp.float32)
    gap = logits[0, ..., 0] - logits[0, ..., 1]
    extra = jnp.stack(
        [named[..., 0], named[..., 1], *thirds(gap), *thirds(difference)], 0
    ).reshape(EXTRA, token_count)
    extra = jnp.pad(extra.astype(jnp.bfloat16), ((0, 0), (0, share - token_count)))

    late = from_next(late)
    direct = {}
    for k in range(2, shares):
        direct[k] = from_next_share(early if k < 3 else after(early, direct[k - 1]), k)
    direct[1] = from_next_share(early, 1)
    zero = from_next(jnp.concatenate([early, extra], 0))
    late_top = swap(late, top)
    direct[0], extra = zero[:cut], zero[cut:]
    zero_top = swap(zero, top)
    direct_top = {0: zero_top[:cut]}
    for k in range(1, shares):
        direct_top[k] = swap(direct[k], top)
    pair = jnp.concatenate([late, late_top, extra], 0)
    pairs = {0: pair}
    for k in range(1, shares):
        pairs[k] = from_share(pair, k)

    def spread(x):
        held, bit = {0: x}, top // 2
        while bit:
            for j in sorted(held):
                held[j ^ bit] = swap(held[j], bit)
            bit //= 2
        return [held[j] for j in sorted(held)]

    extras = spread(jnp.stack([extra[:, :token_count], zero_top[cut:, :token_count]]))
    extras = jnp.concatenate([jnp.stack([e[b] for e in extras]) for b in range(2)], 0)
    extras = extras.astype(jnp.float32).reshape(experts, 8, micros, token_count)
    gap = extras[:, 2] + extras[:, 3] + extras[:, 4]
    weight_first, weight_second = jax.nn.sigmoid(gap), jax.nn.sigmoid(-gap)
    meta = jnp.stack(
        [
            extras[:, 0],
            extras[:, 1],
            jnp.where(received, weight_first, 0.0),
            jnp.where(received, weight_second, 0.0),
        ],
        2,
    ).reshape(experts, 4 * micros, token_count)

    scores = 0.0
    for k in range(shares):
        terms = pairs[k][-EXTRA:, :token_count].astype(jnp.float32)
        terms = terms.reshape(8, micros, token_count)
        scores += terms[5] + terms[6] + terms[7]
    slope = jnp.where(received, weight_first[0] * weight_second[0] * scores, 0.0)
    moved_logits = jnp.stack([slope, -slope], -1).astype(jnp.bfloat16)[None]

    places, weights = find_places(expert.astype(jnp.int32)[None], meta, cap)

    together = 1
    while (share * together) % 128:
        together *= 2
    rows = []
    for part in range(0, shares, together):
        pieces = []
        for k in range(part, part + together):
            block = jnp.concatenate([direct[k], direct_top[k], pairs[k][:-EXTRA]], 0)
            pieces.append(spread(block))
        tokens = pieces[0]
        if together > 1:
            order = jnp.arange(together) ^ (mine % together)
            tokens = []
            for j in range(top):
                stacked = jnp.take(jnp.stack([piece[j] for piece in pieces]), order, axis=0)
                tokens.append(stacked.transpose(1, 0, 2).reshape(-1, together * share))
        rows.append(fill_rows(places, weights, tokens, cut))
    half = len(rows) // 2
    which = mine // together
    total = None
    for side in range(2):
        place = jnp.stack([(which // half) ^ side, which % half]).astype(jnp.int32)
        total = add_part(
            place,
            rows[side * half : (side + 1) * half],
            down_weights,
            total,
            micros,
            experts,
            side == 1,
        )
    return total.transpose(0, 1, 2, 4, 3, 5), moved_logits


def solution(mesh):
    in_specs = (
        P("pipe", None, "expert", "dp"),
        P("pipe", None, "expert", None, "dp"),
        P("pipe", None, "expert", None),
        P("pipe", None, "expert", None),
        P("expert", "dp", None),
    )
    out_specs = (P("pipe", None, "expert", None, None, "dp"), P("pipe", None, "expert", None))
    return jax.shard_map(
        per_device, mesh=mesh, in_specs=in_specs, out_specs=out_specs, check_vma=False
    )
```

```python
import functools

import jax
import jax.numpy as jnp
from jax import lax
from jax.experimental import pallas as pl
from jax.experimental.pallas import tpu as pltpu
from jax.sharding import PartitionSpec as P

MEBI = 1024 * 1024
NT = (((1,), (1,)), ((), ()))
EXTRA = 16


def from_next(x, dp_xor=0):
    sections, shares = lax.axis_size("pipe"), lax.axis_size("dp")
    pairs = [
        (s * shares + z, (s - 1) * shares + (z ^ dp_xor))
        if s
        else (z, (sections - 1) * shares + z)
        for s in range(sections)
        for z in range(shares)
    ]
    return lax.ppermute(x, ("pipe", "dp"), pairs)


def from_share(x, dp_xor, idle):
    sections, shares = lax.axis_size("pipe"), lax.axis_size("dp")
    experts = lax.axis_size("expert")
    pairs = []
    for s in range(sections):
        for z in range(shares):
            for e in range(experts):
                to = (s, z, e ^ 1) if s == idle else (s, z ^ dp_xor, e)
                pairs.append(
                    ((s * shares + z) * experts + e, (to[0] * shares + to[1]) * experts + to[2])
                )
    return lax.ppermute(x, ("pipe", "dp", "expert"), pairs)


def swap(x, bit):
    experts = lax.axis_size("expert")
    return lax.ppermute(x, "expert", [(e, e ^ bit) for e in range(experts)])


def join_kernel(count, *refs):
    out_ref, at = refs[-1], 0
    for ref in refs[:count]:
        out_ref[at : at + ref.shape[0], :] = ref[...]
        at += ref.shape[0]


def join(blocks, gates=()):
    blocks, gates = list(blocks), [gate for gate in gates if gate is not None]
    rows, share = sum(block.shape[0] for block in blocks), blocks[0].shape[1]
    return pl.pallas_call(
        functools.partial(join_kernel, len(blocks)),
        in_specs=[pl.BlockSpec(memory_space=pltpu.VMEM)] * len(blocks)
        + [pl.BlockSpec(memory_space=pl.ANY)] * len(gates),
        out_specs=pl.BlockSpec(memory_space=pltpu.VMEM),
        out_shape=jax.ShapeDtypeStruct((rows, share), blocks[0].dtype),
        compiler_params=pltpu.CompilerParams(vmem_limit_bytes=4 * MEBI),
    )(*blocks, *gates)


def thirds(x):
    high = x.astype(jnp.bfloat16).astype(jnp.float32)
    middle = (x - high).astype(jnp.bfloat16).astype(jnp.float32)
    return [high, middle, x - high - middle]


def meta_kernel(logits_ref, routes_ref, meta_ref):
    micros, _, tokens = logits_ref.shape
    share = meta_ref.shape[1]
    lines = []
    for micro in range(micros):
        routes = routes_ref[micro].astype(jnp.float32)
        gap = logits_ref[micro, 0:1] - logits_ref[micro, 1:2]
        lines += [routes[0:1], routes[1:2], *thirds(gap), *[jnp.zeros_like(gap)] * 3]
    lines = jnp.concatenate(lines, 0)
    if share > tokens:
        lines = jnp.concatenate([lines, jnp.zeros((EXTRA, share - tokens), jnp.float32)], 1)
    meta_ref[...] = lines.astype(jnp.bfloat16)


def score_kernel(scores_ref, rows_ref):
    micros, tokens = scores_ref.shape
    share = rows_ref.shape[1]
    lines = jnp.concatenate(thirds(scores_ref[...]), 0)
    lines = jnp.concatenate([lines, jnp.zeros((EXTRA - 3 * micros, tokens), jnp.float32)], 0)
    if share > tokens:
        lines = jnp.concatenate([lines, jnp.zeros((EXTRA, share - tokens), jnp.float32)], 1)
    rows_ref[...] = lines.astype(jnp.bfloat16)


def extra_rows(kernel, share, *args):
    in_vmem = pl.BlockSpec(memory_space=pltpu.VMEM)
    return pl.pallas_call(
        kernel,
        in_specs=[in_vmem] * len(args),
        out_specs=in_vmem,
        out_shape=jax.ShapeDtypeStruct((EXTRA, share), jnp.bfloat16),
        compiler_params=pltpu.CompilerParams(vmem_limit_bytes=4 * MEBI),
    )(*args)


def place_kernel(expert_ref, meta_ref, places_ref, weights_ref):
    expert = expert_ref[0]
    groups, _, tokens = meta_ref.shape
    micros = meta_ref.shape[1] // 4
    rows = places_ref.shape[1]
    earlier = lax.broadcasted_iota(jnp.int32, (tokens, tokens), 0) < lax.broadcasted_iota(
        jnp.int32, (tokens, tokens), 1
    )
    earlier = earlier.astype(jnp.bfloat16)
    row = lax.broadcasted_iota(jnp.int32, (rows, tokens), 0)
    weights = []
    for micro in range(micros):
        for j in range(groups):
            meta = meta_ref[j]
            first = meta[4 * micro : 4 * micro + 1] == expert.astype(jnp.float32)
            second = meta[4 * micro + 1 : 4 * micro + 2] == expert.astype(jnp.float32)
            here = jnp.logical_or(first, second)
            weights.append(
                jnp.where(
                    first, meta[4 * micro + 2 : 4 * micro + 3], meta[4 * micro + 3 : 4 * micro + 4]
                )
            )
            named = jnp.broadcast_to(here.astype(jnp.float32), (16, tokens)).astype(jnp.bfloat16)
            slot = jnp.dot(named, earlier, preferred_element_type=jnp.float32)[0:1]
            target = slot.astype(jnp.int32) * groups + (expert ^ j)
            picked = row == jnp.where(here, target, -1)
            places_ref[micro, :, j * tokens : (j + 1) * tokens] = picked.astype(
                jnp.float32
            ).astype(jnp.bfloat16)
    weights = jnp.concatenate(weights, 0)
    padding = jnp.zeros((tokens - weights.shape[0], tokens), jnp.float32)
    weights_ref[...] = jnp.transpose(jnp.concatenate([weights, padding], 0))


def find_places(expert, meta, cap):
    groups, quads, tokens = meta.shape
    micros = quads // 4
    in_vmem = pl.BlockSpec(memory_space=pltpu.VMEM)
    return pl.pallas_call(
        place_kernel,
        in_specs=[pl.BlockSpec(memory_space=pltpu.SMEM), in_vmem],
        out_specs=[in_vmem, in_vmem],
        out_shape=[
            jax.ShapeDtypeStruct((micros, cap * groups, groups * tokens), jnp.bfloat16),
            jax.ShapeDtypeStruct((tokens, tokens), jnp.float32),
        ],
        compiler_params=pltpu.CompilerParams(vmem_limit_bytes=16 * MEBI),
    )(expert, meta)


def fill_kernel(cut, count, places_ref, weights_ref, *refs):
    token_refs, rows_ref = refs[:count], refs[-1]
    micros, rows, _ = places_ref.shape
    tokens = weights_ref.shape[0]
    late = micros * tokens - cut
    for micro in range(micros):
        blocks = []
        for j in range(2 * count):
            source, top = token_refs[j % count], j // count
            low, high = micro * tokens, (micro + 1) * tokens
            pieces = []
            if low < cut:
                pieces.append(source[top * cut + low : top * cut + min(high, cut), :])
            if high > cut:
                at = 2 * cut + top * late - cut
                pieces.append(source[at + max(low, cut) : at + high, :])
            held = pieces[0] if len(pieces) == 1 else jnp.concatenate(pieces, 0)
            weight = weights_ref[:, micro * 2 * count + j : micro * 2 * count + j + 1]
            blocks.append((held.astype(jnp.float32) * weight).astype(jnp.bfloat16))
        rows_ref[micro * rows : (micro + 1) * rows, :] = jnp.dot(
            places_ref[micro], jnp.concatenate(blocks, 0), preferred_element_type=jnp.float32
        ).astype(jnp.bfloat16)


def fill_rows(places, weights, tokens, cut, gates):
    micros, rows, _ = places.shape
    depth = tokens[0].shape[1]
    in_vmem = pl.BlockSpec(memory_space=pltpu.VMEM)
    return pl.pallas_call(
        functools.partial(fill_kernel, cut, len(tokens)),
        in_specs=[in_vmem] * (2 + len(tokens))
        + [pl.BlockSpec(memory_space=pl.ANY)] * len(gates),
        out_specs=in_vmem,
        out_shape=jax.ShapeDtypeStruct((micros * rows, depth), jnp.bfloat16),
        compiler_params=pltpu.CompilerParams(vmem_limit_bytes=12 * MEBI),
    )(places, weights, *tokens, *gates)


def part_kernel(parts, groups, first, last, *refs):
    row_refs = refs[1 : 1 + parts]
    weight_refs = refs[1 + parts : 1 + 2 * parts]
    rest = refs[1 + 2 * parts :]
    product = None
    for row_ref, weight_ref in zip(row_refs, weight_refs):
        term = lax.dot_general(
            row_ref[...], weight_ref[0], NT, preferred_element_type=jnp.float32
        )
        product = term if product is None else product + term
    block = product.shape[1]
    here = pl.ds(pl.multiple_of(pl.program_id(0) * block, block), block)
    if not first:
        product = product + rest[0][:, here]
    if not last:
        rest[-2][:, here] = product
        rest[-1][...] = product[:8, :128]
    else:
        out_ref = rest[-1]
        micros, cap = out_ref.shape[1], out_ref.shape[3]
        rows = cap * groups
        for micro in range(micros):
            out_ref[0, micro, 0] = (
                product[micro * rows : (micro + 1) * rows]
                .astype(out_ref.dtype)
                .reshape(cap, groups, block)
            )


def add_parts(place, begin, rows, weights, total, micros, groups, last):
    count, depth = rows[0].shape
    hidden = weights.shape[1]
    block = min(1024, hidden)
    in_vmem = pl.BlockSpec(memory_space=pltpu.VMEM)
    in_specs = [in_vmem] * len(rows)
    for i in range(begin, begin + len(rows)):
        in_specs.append(pl.BlockSpec((1, block, depth), lambda f, p, i=i: (0, f, p[i])))
    weights = pltpu.with_memory_space_constraint(weights, pltpu.HBM)
    args = [place, *rows, *[weights] * len(rows)]
    if total is not None:
        in_specs.append(in_vmem)
        args.append(total)
    if last:
        cap = count // (micros * groups)
        out_shape = jax.ShapeDtypeStruct((1, micros, 1, cap, groups, hidden), jnp.bfloat16)
        out_spec = pl.BlockSpec(
            (1, micros, 1, cap, groups, block), lambda f, p: (0, 0, 0, 0, 0, f)
        )
    else:
        out_shape = [
            jax.ShapeDtypeStruct((count, hidden), jnp.float32),
            jax.ShapeDtypeStruct((8, 128), jnp.float32),
        ]
        out_spec = [in_vmem, in_vmem]
    return pl.pallas_call(
        functools.partial(part_kernel, len(rows), groups, total is None, last),
        grid_spec=pltpu.PrefetchScalarGridSpec(
            num_scalar_prefetch=1,
            grid=(hidden // block,),
            in_specs=in_specs,
            out_specs=out_spec,
        ),
        out_shape=out_shape,
        compiler_params=pltpu.CompilerParams(vmem_limit_bytes=24 * MEBI),
        cost_estimate=pl.CostEstimate(
            flops=2 * count * depth * len(rows) * hidden,
            bytes_accessed=2 * hidden * depth * len(rows),
            transcendentals=0,
        ),
    )(*args)


def per_device(out_grad, expert_outputs, logits, routes, down_weights):
    micros, token_count, share = out_grad.shape[1:]
    experts, shares = lax.axis_size("expert"), lax.axis_size("dp")
    cap = min(token_count, 2 * token_count // experts + token_count // 32)
    expert, mine = lax.axis_index("expert"), lax.axis_index("dp")
    sections = lax.axis_size("pipe")
    received = lax.axis_index("pipe") < sections - 1
    top = experts // 2
    cut = micros * token_count * 11 // 16
    own = out_grad.reshape(micros * token_count, share)
    early, late = own[:cut], own[cut:]
    meta = extra_rows(
        meta_kernel, share, logits[0].transpose(0, 2, 1), routes[0].transpose(0, 2, 1)
    )

    late = from_next(late)
    direct = {2: from_next(early, 2)}
    late_top = swap(late, top)
    zero = from_next(join([early, meta], [late]))
    zero_top = swap(zero, top)
    direct[0], direct_top = zero[:cut], {0: zero_top[:cut]}
    direct[1] = from_next(join([early], [zero]), 1)

    grads, outputs = out_grad[0].astype(jnp.float32), expert_outputs[0].astype(jnp.float32)
    scores = jnp.sum(grads * (outputs[:, :, 0] - outputs[:, :, 1]), -1)
    step = 1
    while step < shares:
        scores += from_share(scores, step, 0)
        step *= 2
    scores = extra_rows(score_kernel, share, scores)

    pair = join([late, late_top])
    pairs = {0: pair, 2: from_share(pair, 2, sections - 1), 1: from_share(pair, 1, sections - 1)}
    for k in range(3, shares):
        sent = [early] if k < shares - 1 else [early, scores]
        direct[k] = from_next(join(sent, [direct[k - 1]]), k)
    scores, direct[shares - 1] = direct[shares - 1][cut:], direct[shares - 1][:cut]
    for k in range(1, shares):
        direct_top[k] = swap(direct[k], top)
    for k in range(3, shares):
        pairs[k] = from_share(join([pair], [pairs[k - 2]]), k, sections - 1)

    def spread(x):
        held, bit = {0: x}, top // 2
        while bit:
            for j in sorted(held):
                held[j ^ bit] = swap(held[j], bit)
            bit //= 2
        return [held[j] for j in sorted(held)]

    extras = spread(jnp.stack([x[-EXTRA:, :token_count] for x in (zero, zero_top)]))
    extras = jnp.concatenate([jnp.stack([e[b] for e in extras]) for b in range(2)], 0)
    extras = extras.astype(jnp.float32).reshape(experts, micros, 8, token_count)
    extras = extras.transpose(0, 2, 1, 3)
    gap = extras[:, 2] + extras[:, 3] + extras[:, 4]
    weight_first, weight_second = jax.nn.sigmoid(gap), jax.nn.sigmoid(-gap)
    meta = jnp.stack(
        [
            extras[:, 0],
            extras[:, 1],
            jnp.where(received, weight_first, 0.0),
            jnp.where(received, weight_second, 0.0),
        ],
        2,
    ).reshape(experts, 4 * micros, token_count)

    scores = scores[: 3 * micros, :token_count].astype(jnp.float32)
    scores = scores.reshape(3, micros, token_count)
    scores = scores[0] + scores[1] + scores[2]
    slope = jnp.where(received, weight_first[0] * weight_second[0] * scores, 0.0)
    moved_logits = jnp.stack([slope, -slope], -1).astype(jnp.bfloat16)[None]

    places, weights = find_places(expert.astype(jnp.int32)[None], meta, cap)

    together = 1
    while (share * together) % 128:
        together *= 2
    rows = []
    for which in range(shares // together):
        pieces = []
        for k in range(which * together, (which + 1) * together):
            pieces.append(spread(join([direct[k], direct_top[k], pairs[k]])))
        tokens = pieces[0]
        if together > 1:
            order = jnp.arange(together) ^ (mine % together)
            tokens = []
            for j in range(top):
                stacked = jnp.take(jnp.stack([piece[j] for piece in pieces]), order, axis=0)
                tokens.append(stacked.transpose(1, 0, 2).reshape(-1, together * share))
        rows.append(fill_rows(places, weights, tokens, cut, []))
    place = jnp.stack([(mine // together) ^ i for i in range(len(rows))]).astype(jnp.int32)
    hidden = add_parts(place, 0, rows, down_weights, None, micros, experts, True)
    return hidden.transpose(0, 1, 2, 4, 3, 5), moved_logits


def solution(mesh):
    in_specs = (
        P("pipe", None, "expert", "dp"),
        P("pipe", None, "expert", None, "dp"),
        P("pipe", None, "expert", None),
        P("pipe", None, "expert", None),
        P("expert", "dp", None),
    )
    out_specs = (P("pipe", None, "expert", None, None, "dp"), P("pipe", None, "expert", None))
    return jax.shard_map(
        per_device, mesh=mesh, in_specs=in_specs, out_specs=out_specs, check_vma=False
    )
```

```python
import functools

import jax
import jax.numpy as jnp
from jax import lax
from jax.experimental import pallas as pl
from jax.experimental.pallas import tpu as pltpu
from jax.sharding import PartitionSpec as P

MEBI = 1024 * 1024
NT = (((1,), (1,)), ((), ()))
EXTRA = 16
COPIES = 4


def from_next(x, dp_xor=0):
    sections, shares = lax.axis_size("pipe"), lax.axis_size("dp")
    pairs = [
        (s * shares + z, (s - 1) * shares + (z ^ dp_xor))
        if s
        else (z, (sections - 1) * shares + z)
        for s in range(sections)
        for z in range(shares)
    ]
    return lax.ppermute(x, ("pipe", "dp"), pairs)


def from_share(x, dp_xor, idle):
    sections, shares = lax.axis_size("pipe"), lax.axis_size("dp")
    experts = lax.axis_size("expert")
    pairs = []
    for s in range(sections):
        for z in range(shares):
            for e in range(experts):
                to = (s, z, e ^ 1) if s == idle else (s, z ^ dp_xor, e)
                pairs.append(
                    ((s * shares + z) * experts + e, (to[0] * shares + to[1]) * experts + to[2])
                )
    return lax.ppermute(x, ("pipe", "dp", "expert"), pairs)


def swap(x, bit):
    experts = lax.axis_size("expert")
    return lax.ppermute(x, "expert", [(e, e ^ bit) for e in range(experts)])


def join_kernel(count, *refs):
    out_ref, at = refs[-1], 0
    for ref in refs[:count]:
        out_ref[at : at + ref.shape[0], :] = ref[...]
        at += ref.shape[0]


def join(blocks, gates=()):
    blocks, gates = list(blocks), [gate for gate in gates if gate is not None]
    rows, share = sum(block.shape[0] for block in blocks), blocks[0].shape[1]
    return pl.pallas_call(
        functools.partial(join_kernel, len(blocks)),
        in_specs=[pl.BlockSpec(memory_space=pltpu.VMEM)] * len(blocks)
        + [pl.BlockSpec(memory_space=pl.ANY)] * len(gates),
        out_specs=pl.BlockSpec(memory_space=pltpu.VMEM),
        out_shape=jax.ShapeDtypeStruct((rows, share), blocks[0].dtype),
        compiler_params=pltpu.CompilerParams(vmem_limit_bytes=4 * MEBI),
    )(*blocks, *gates)


def thirds(x):
    high = x.astype(jnp.bfloat16).astype(jnp.float32)
    middle = (x - high).astype(jnp.bfloat16).astype(jnp.float32)
    return [high, middle, x - high - middle]


def extra_kernel(_, *refs):
    extra_ref, held, done = refs[4], refs[5:9], refs[9]
    copies = [pltpu.make_async_copy(refs[i], held[i], done.at[i]) for i in range(4)]
    for copy in copies:
        copy.start()
    for copy in copies:
        copy.wait()
    logits_ref, routes_ref, grads_ref, outputs_ref = held
    micros, _, tokens = logits_ref.shape
    share = extra_ref.shape[1]
    pair = lax.broadcasted_iota(jnp.int32, (2 * tokens, tokens), 0)
    token = lax.broadcasted_iota(jnp.int32, (2 * tokens, tokens), 1)
    lines = []
    for micro in range(micros):
        routes = routes_ref[micro].astype(jnp.float32)
        gap = logits_ref[micro, 0:1] - logits_ref[micro, 1:2]
        products = lax.dot_general(
            outputs_ref[micro].reshape(2 * tokens, share),
            grads_ref[micro],
            NT,
            preferred_element_type=jnp.float32,
        )
        first = jnp.sum(jnp.where(pair == 2 * token, products, 0.0), 0, keepdims=True)
        second = jnp.sum(jnp.where(pair == 2 * token + 1, products, 0.0), 0, keepdims=True)
        lines += [routes[0:1], routes[1:2], *thirds(gap), *thirds(first - second)]
    lines = jnp.concatenate(lines, 0)
    if share > tokens:
        lines = jnp.concatenate([lines, jnp.zeros((EXTRA, share - tokens), jnp.float32)], 1)
    extra_ref[...] = lines.astype(jnp.bfloat16)


def extra_rows(share, flags, *args):
    return pl.pallas_call(
        extra_kernel,
        in_specs=[pl.BlockSpec(memory_space=pltpu.SMEM)]
        + [pl.BlockSpec(memory_space=pltpu.HBM)] * len(args),
        out_specs=pl.BlockSpec(memory_space=pltpu.VMEM),
        out_shape=jax.ShapeDtypeStruct((EXTRA, share), jnp.bfloat16),
        scratch_shapes=[pltpu.VMEM(arg.shape, arg.dtype) for arg in args]
        + [pltpu.SemaphoreType.DMA((len(args),))],
        compiler_params=pltpu.CompilerParams(vmem_limit_bytes=4 * MEBI),
    )(flags, *[pltpu.with_memory_space_constraint(arg, pltpu.HBM) for arg in args])


def place_kernel(flags_ref, meta_ref, places_ref, weights_ref, kept_ref):
    expert, received = flags_ref[0], flags_ref[1].astype(jnp.float32)
    groups, _, tokens = meta_ref.shape
    micros = meta_ref.shape[1] // 4
    rows = places_ref.shape[1]
    earlier = lax.broadcasted_iota(jnp.int32, (tokens, tokens), 0) < lax.broadcasted_iota(
        jnp.int32, (tokens, tokens), 1
    )
    earlier = earlier.astype(jnp.bfloat16)
    row = lax.broadcasted_iota(jnp.int32, (rows, tokens), 0)
    weights = []
    for micro in range(micros):
        for j in range(groups):
            meta = meta_ref[j]
            first = meta[4 * micro : 4 * micro + 1] == expert.astype(jnp.float32)
            second = meta[4 * micro + 1 : 4 * micro + 2] == expert.astype(jnp.float32)
            here = jnp.logical_or(first, second)
            weights.append(
                jnp.where(
                    first, meta[4 * micro + 2 : 4 * micro + 3], meta[4 * micro + 3 : 4 * micro + 4]
                )
            )
            named = jnp.broadcast_to(here.astype(jnp.float32), (16, tokens)).astype(jnp.bfloat16)
            slot = jnp.dot(named, earlier, preferred_element_type=jnp.float32)[0:1]
            target = slot.astype(jnp.int32) * groups + (expert ^ j)
            picked = row == jnp.where(here, target, -1)
            places_ref[micro, :, j * tokens : (j + 1) * tokens] = picked.astype(
                jnp.float32
            ).astype(jnp.bfloat16)
    weights = jnp.concatenate(weights, 0)
    padding = jnp.zeros((tokens - weights.shape[0], tokens), jnp.float32)
    weights_ref[...] = jnp.transpose(jnp.concatenate([weights * received, padding], 0))
    kept_ref[...] = jnp.zeros_like(kept_ref) + received


def find_places(flags, meta, cap):
    groups, quads, tokens = meta.shape
    micros = quads // 4
    in_vmem = pl.BlockSpec(memory_space=pltpu.VMEM)
    return pl.pallas_call(
        place_kernel,
        in_specs=[pl.BlockSpec(memory_space=pltpu.SMEM), in_vmem],
        out_specs=[in_vmem] * 3,
        out_shape=[
            jax.ShapeDtypeStruct((micros, cap * groups, groups * tokens), jnp.bfloat16),
            jax.ShapeDtypeStruct((tokens, tokens), jnp.float32),
            jax.ShapeDtypeStruct((micros, tokens), jnp.float32),
        ],
        compiler_params=pltpu.CompilerParams(vmem_limit_bytes=16 * MEBI),
    )(flags, meta)


def fill_kernel(cut, count, places_ref, weights_ref, *refs):
    token_refs, rows_ref = refs[:count], refs[-1]
    micros, rows, _ = places_ref.shape
    tokens = weights_ref.shape[0]
    late = micros * tokens - cut
    for micro in range(micros):
        blocks = []
        for j in range(2 * count):
            source, top = token_refs[j % count], j // count
            low, high = micro * tokens, (micro + 1) * tokens
            pieces = []
            if low < cut:
                pieces.append(source[top * cut + low : top * cut + min(high, cut), :])
            if high > cut:
                at = 2 * cut + top * late - cut
                pieces.append(source[at + max(low, cut) : at + high, :])
            held = pieces[0] if len(pieces) == 1 else jnp.concatenate(pieces, 0)
            weight = weights_ref[:, micro * 2 * count + j : micro * 2 * count + j + 1]
            blocks.append((held.astype(jnp.float32) * weight).astype(jnp.bfloat16))
        rows_ref[micro * rows : (micro + 1) * rows, :] = jnp.dot(
            places_ref[micro], jnp.concatenate(blocks, 0), preferred_element_type=jnp.float32
        ).astype(jnp.bfloat16)


def fill_rows(places, weights, tokens, cut, gates):
    micros, rows, _ = places.shape
    depth = tokens[0].shape[1]
    in_vmem = pl.BlockSpec(memory_space=pltpu.VMEM)
    return pl.pallas_call(
        functools.partial(fill_kernel, cut, len(tokens)),
        in_specs=[in_vmem] * (2 + len(tokens))
        + [pl.BlockSpec(memory_space=pl.ANY)] * len(gates),
        out_specs=in_vmem,
        out_shape=jax.ShapeDtypeStruct((micros * rows, depth), jnp.bfloat16),
        compiler_params=pltpu.CompilerParams(vmem_limit_bytes=12 * MEBI),
    )(places, weights, *tokens, *gates)


def column_copies(weights_hbm, share, held_ref, done):
    hidden, depth = held_ref.shape
    block = hidden // done.shape[0]
    columns = pl.ds(pl.multiple_of(share * depth, 128), depth)
    return [
        pltpu.make_async_copy(
            weights_hbm.at[0, pl.ds(i * block, block), columns],
            held_ref.at[pl.ds(i * block, block), :],
            done.at[i],
        )
        for i in range(done.shape[0])
    ]


def fetch_kernel(index, flags_ref, weights_hbm, *refs):
    held_ref, done = refs[-2:]
    copies = column_copies(weights_hbm, flags_ref[index], held_ref, done)
    for copy in copies:
        copy.start()
    for copy in copies:
        copy.wait()


def fetch(flags, index, weights, depth, gates):
    return pl.pallas_call(
        functools.partial(fetch_kernel, index),
        in_specs=[pl.BlockSpec(memory_space=pltpu.SMEM), pl.BlockSpec(memory_space=pltpu.HBM)]
        + [pl.BlockSpec(memory_space=pl.ANY)] * len(gates),
        out_specs=pl.BlockSpec(memory_space=pltpu.VMEM),
        out_shape=jax.ShapeDtypeStruct((weights.shape[1], depth), weights.dtype),
        scratch_shapes=[pltpu.SemaphoreType.DMA((COPIES,))],
        compiler_params=pltpu.CompilerParams(vmem_limit_bytes=1 * MEBI),
    )(flags, pltpu.with_memory_space_constraint(weights, pltpu.HBM), *gates)


def multiply(row_refs, weight_refs, here):
    product = None
    for row_ref, weight_ref in zip(row_refs, weight_refs):
        term = lax.dot_general(
            row_ref[...], weight_ref[here, :], NT, preferred_element_type=jnp.float32
        )
        product = term if product is None else product + term
    return product


def first_kernel(block, count, following, flags_ref, weights_hbm, *refs):
    row_refs, weight_refs, rest = refs[:count], refs[count : 2 * count], refs[2 * count :]
    total_ref, token_ref, later_refs, done = rest[0], rest[1], rest[2:-1], rest[-1]
    copies = []
    for i, later_ref in enumerate(later_refs):
        copies += column_copies(weights_hbm, flags_ref[following + i], later_ref, done.at[i])
    for copy in copies:
        copy.start()

    @pl.loop(0, total_ref.shape[1] // block)
    def _(step):
        here = pl.ds(pl.multiple_of(step * block, block), block)
        total_ref[:, here] = multiply(row_refs, weight_refs, here)

    token_ref[...] = total_ref[:8, :128]
    for copy in copies:
        copy.wait()


def multiply_first(flags, following, later, rows, held, weights):
    count, depth = rows[0].shape
    hidden = weights.shape[1]
    in_vmem = pl.BlockSpec(memory_space=pltpu.VMEM)
    outs = pl.pallas_call(
        functools.partial(first_kernel, min(1024, hidden), len(rows), following),
        in_specs=[pl.BlockSpec(memory_space=pltpu.SMEM), pl.BlockSpec(memory_space=pltpu.HBM)]
        + [in_vmem] * (2 * len(rows)),
        out_specs=[in_vmem] * (2 + later),
        out_shape=[
            jax.ShapeDtypeStruct((count, hidden), jnp.float32),
            jax.ShapeDtypeStruct((8, 128), jnp.float32),
        ]
        + [jax.ShapeDtypeStruct((hidden, depth), weights.dtype)] * later,
        scratch_shapes=[pltpu.SemaphoreType.DMA((later, COPIES))],
        compiler_params=pltpu.CompilerParams(vmem_limit_bytes=12 * MEBI),
        cost_estimate=pl.CostEstimate(
            flops=2 * count * depth * len(rows) * hidden,
            bytes_accessed=2 * hidden * depth * len(rows),
            transcendentals=0,
        ),
    )(flags, pltpu.with_memory_space_constraint(weights, pltpu.HBM), *rows, *held)
    return outs[0], outs[1], outs[2:]


def last_kernel(groups, count, *refs):
    row_refs, weight_refs = refs[:count], refs[count : 2 * count]
    total_ref, out_ref = refs[2 * count :]
    micros, cap, block = out_ref.shape[1], out_ref.shape[3], out_ref.shape[5]
    here = pl.ds(pl.multiple_of(pl.program_id(0) * block, block), block)
    product = multiply(row_refs, weight_refs, here) + total_ref[:, here]
    rows = cap * groups
    for micro in range(micros):
        out_ref[0, micro, 0] = (
            product[micro * rows : (micro + 1) * rows]
            .astype(out_ref.dtype)
            .reshape(cap, groups, block)
        )


def multiply_last(rows, held, total, micros, groups):
    count, hidden = total.shape
    depth = rows[0].shape[1]
    block = min(1024, hidden)
    cap = count // (micros * groups)
    in_vmem = pl.BlockSpec(memory_space=pltpu.VMEM)
    return pl.pallas_call(
        functools.partial(last_kernel, groups, len(rows)),
        grid=(hidden // block,),
        in_specs=[in_vmem] * (2 * len(rows) + 1),
        out_specs=pl.BlockSpec((1, micros, 1, cap, groups, block), lambda f: (0, 0, 0, 0, 0, f)),
        out_shape=jax.ShapeDtypeStruct((1, micros, 1, cap, groups, hidden), jnp.bfloat16),
        compiler_params=pltpu.CompilerParams(vmem_limit_bytes=16 * MEBI),
        cost_estimate=pl.CostEstimate(
            flops=2 * count * depth * len(rows) * hidden,
            bytes_accessed=2 * hidden * depth * len(rows),
            transcendentals=0,
        ),
    )(*rows, *held, total)


def per_device(out_grad, expert_outputs, logits, routes, down_weights):
    micros, token_count, share = out_grad.shape[1:]
    experts, shares = lax.axis_size("expert"), lax.axis_size("dp")
    cap = min(token_count, 2 * token_count // experts + token_count // 32)
    expert, mine = lax.axis_index("expert"), lax.axis_index("dp")
    sections = lax.axis_size("pipe")
    received = lax.axis_index("pipe") < sections - 1
    together = 1
    while (share * together) % 128:
        together *= 2
    sets = list(range(shares // together))
    half = len(sets) // 2
    gated = sets[half:]
    if together == 1:
        sets, half, gated = [2,0,1,3, *sets[4:]], 2, [1, 3]
    flags = jnp.stack([expert, received, *[(mine // together) ^ which for which in sets]])
    flags = flags.astype(jnp.int32)
    top = experts // 2
    cut = micros * token_count * 11 // 16
    own = out_grad.reshape(micros * token_count, share)
    early, late = own[:cut], own[cut:]
    late = from_next(late)
    direct = {2: from_next(early, 2)}
    late_top = swap(late, top)

    extra = extra_rows(
        share,
        flags,
        logits[0].transpose(0, 2, 1),
        routes[0].transpose(0, 2, 1),
        out_grad[0],
        expert_outputs[0],
    )
    extras = {}
    direct[0] = from_next(join([early, extra], [late]))
    direct[1] = from_next(join([early, extra], [direct[0]]), 1)
    pair = join([late, late_top])
    pairs = {0: pair, 2: from_share(pair, 2, sections - 1), 1: from_share(pair, 1, sections - 1)}
    for k in range(3, shares):
        direct[k] = from_next(join([early, extra], [direct[k - 1]]), k)
        pairs[k] = from_share(join([pair], [pairs[k - 2]]), k, sections - 1)
    near = from_next(join([extra], [direct[shares - 1]]), 2)
    zero_top = swap(direct[0], top)
    direct_top = {0: zero_top[:cut]}
    for k in range(shares):
        if k != 2:
            direct[k], extras[k] = direct[k][:cut], direct[k][cut:]
        if k:
            direct_top[k] = swap(direct[k], top)

    def spread(x):
        held, bit = {0: x}, top // 2
        while bit:
            for j in sorted(held):
                held[j ^ bit] = swap(held[j], bit)
            bit //= 2
        return [held[j] for j in sorted(held)]

    metas = spread(jnp.stack([x[:, :token_count] for x in (extras[0], zero_top[cut:])]))
    metas = jnp.concatenate([jnp.stack([m[b] for m in metas]) for b in range(2)], 0)
    metas = metas.astype(jnp.float32).reshape(experts, micros, 8, token_count)
    gap = metas[:, :, 2] + metas[:, :, 3] + metas[:, :, 4]
    weight_first, weight_second = jax.nn.sigmoid(gap), jax.nn.sigmoid(-gap)
    meta = jnp.stack(
        [
            metas[:, :, 0],
            metas[:, :, 1],
            weight_first,
            weight_second,
        ],
        2,
    ).reshape(experts, 4 * micros, token_count)

    places, weights, kept = find_places(flags, meta, cap)
    def filled(which, gates, fill_gates):
        pieces = []
        for k in range(which * together, (which + 1) * together):
            pieces.append(spread(join([direct[k], direct_top[k], pairs[k]], gates)))
        tokens = pieces[0]
        if together > 1:
            order = jnp.arange(together) ^ (mine % together)
            tokens = []
            for j in range(top):
                stacked = jnp.take(jnp.stack([piece[j] for piece in pieces]), order, axis=0)
                tokens.append(stacked.transpose(1, 0, 2).reshape(-1, together * share))
        return fill_rows(places, weights, tokens, cut, fill_gates)

    fetch_gates = [[pairs[2]], [pairs[2]]]
    held = []
    for i in range(half):
        gates = fetch_gates[i] if i < len(fetch_gates) else []
        held.append(fetch(flags, 2 + i, down_weights, together * share, gates))
    rows = [filled(which, [], []) for which in sets[:half]]
    total, done, held = multiply_first(
        flags, 2 + half, len(sets) - half, rows, held, down_weights
    )
    extras[2] = join([near], [done])
    scores = 0.0
    for k in range(shares):
        terms = extras[k][:, :token_count].astype(jnp.float32).reshape(micros, 8, token_count)
        scores += terms[:, 5] + terms[:, 6] + terms[:, 7]
    slope = jnp.where(kept > 0, weight_first[0] * weight_second[0] * scores, 0.0)
    moved_logits = jnp.stack([slope, -slope], -1).astype(jnp.bfloat16)[None]

    rows = [filled(which, [done] if which in gated else [], []) for which in sets[half:]]
    hidden = multiply_last(rows, held, total, micros, experts)
    return hidden.transpose(0, 1, 2, 4, 3, 5), moved_logits


def solution(mesh):
    in_specs = (
        P("pipe", None, "expert", "dp"),
        P("pipe", None, "expert", None, "dp"),
        P("pipe", None, "expert", None),
        P("pipe", None, "expert", None),
        P("expert", "dp", None),
    )
    out_specs = (P("pipe", None, "expert", None, None, "dp"), P("pipe", None, "expert", None))
    return jax.shard_map(
        per_device, mesh=mesh, in_specs=in_specs, out_specs=out_specs, check_vma=False
    )
```

```python
import functools

import jax
import jax.numpy as jnp
from jax import lax
from jax.experimental import pallas as pl
from jax.experimental.pallas import tpu as pltpu
from jax.sharding import PartitionSpec as P

MEBI = 1024 * 1024
NT = (((1,), (1,)), ((), ()))
EXTRA = 16
COPIES = 4


def from_next(x, dp_xor=0):
    sections, shares = lax.axis_size("pipe"), lax.axis_size("dp")
    pairs = [
        (s * shares + z, (s - 1) * shares + (z ^ dp_xor))
        if s
        else (z, (sections - 1) * shares + z)
        for s in range(sections)
        for z in range(shares)
    ]
    return lax.ppermute(x, ("pipe", "dp"), pairs)


def from_share(x, dp_xor, idle):
    sections, shares = lax.axis_size("pipe"), lax.axis_size("dp")
    experts = lax.axis_size("expert")
    pairs = []
    for s in range(sections):
        for z in range(shares):
            for e in range(experts):
                to = (s, z, e ^ 1) if s == idle else (s, z ^ dp_xor, e)
                pairs.append(
                    ((s * shares + z) * experts + e, (to[0] * shares + to[1]) * experts + to[2])
                )
    return lax.ppermute(x, ("pipe", "dp", "expert"), pairs)


def swap(x, bit):
    experts = lax.axis_size("expert")
    return lax.ppermute(x, "expert", [(e, e ^ bit) for e in range(experts)])


def join_kernel(count, *refs):
    out_ref, at = refs[-1], 0
    for ref in refs[:count]:
        out_ref[at : at + ref.shape[0], :] = ref[...]
        at += ref.shape[0]


def join(blocks, gates=()):
    blocks, gates = list(blocks), [gate for gate in gates if gate is not None]
    rows, share = sum(block.shape[0] for block in blocks), blocks[0].shape[1]
    return pl.pallas_call(
        functools.partial(join_kernel, len(blocks)),
        in_specs=[pl.BlockSpec(memory_space=pltpu.VMEM)] * len(blocks)
        + [pl.BlockSpec(memory_space=pl.ANY)] * len(gates),
        out_specs=pl.BlockSpec(memory_space=pltpu.VMEM),
        out_shape=jax.ShapeDtypeStruct((rows, share), blocks[0].dtype),
        compiler_params=pltpu.CompilerParams(vmem_limit_bytes=4 * MEBI),
    )(*blocks, *gates)


def thirds(x):
    high = x.astype(jnp.bfloat16).astype(jnp.float32)
    middle = (x - high).astype(jnp.bfloat16).astype(jnp.float32)
    return [high, middle, x - high - middle]


def extra_kernel(*refs):
    extra_ref, held, done = refs[-6], refs[-5:-1], refs[-1]
    copies = [pltpu.make_async_copy(refs[i], held[i], done.at[i]) for i in range(4)]
    for copy in copies:
        copy.start()
    for copy in copies:
        copy.wait()
    logits_ref, routes_ref, grads_ref, outputs_ref = held
    micros, _, tokens = logits_ref.shape
    share = extra_ref.shape[1]
    pair = lax.broadcasted_iota(jnp.int32, (2 * tokens, tokens), 0)
    token = lax.broadcasted_iota(jnp.int32, (2 * tokens, tokens), 1)
    lines = []
    for micro in range(micros):
        routes = routes_ref[micro].astype(jnp.float32)
        gap = logits_ref[micro, 0:1] - logits_ref[micro, 1:2]
        products = lax.dot_general(
            outputs_ref[micro].reshape(2 * tokens, share),
            grads_ref[micro],
            NT,
            preferred_element_type=jnp.float32,
        )
        first = jnp.sum(jnp.where(pair == 2 * token, products, 0.0), 0, keepdims=True)
        second = jnp.sum(jnp.where(pair == 2 * token + 1, products, 0.0), 0, keepdims=True)
        lines += [routes[0:1], routes[1:2], *thirds(gap), *thirds(first - second)]
    lines = jnp.concatenate(lines, 0)
    if share > tokens:
        lines = jnp.concatenate([lines, jnp.zeros((EXTRA, share - tokens), jnp.float32)], 1)
    extra_ref[...] = lines.astype(jnp.bfloat16)


def extra_rows(share, gates, *args):
    return pl.pallas_call(
        extra_kernel,
        in_specs=[pl.BlockSpec(memory_space=pltpu.HBM)] * len(args)
        + [pl.BlockSpec(memory_space=pl.ANY)] * len(gates),
        out_specs=pl.BlockSpec(memory_space=pltpu.VMEM),
        out_shape=jax.ShapeDtypeStruct((EXTRA, share), jnp.bfloat16),
        scratch_shapes=[pltpu.VMEM(arg.shape, arg.dtype) for arg in args]
        + [pltpu.SemaphoreType.DMA((len(args),))],
        compiler_params=pltpu.CompilerParams(vmem_limit_bytes=4 * MEBI),
    )(*[pltpu.with_memory_space_constraint(arg, pltpu.HBM) for arg in args], *gates)


def place_kernel(meta_ref, places_ref, weights_ref, kept_ref):
    expert = lax.axis_index("expert")
    received = lax.axis_index("pipe") < lax.axis_size("pipe") - 1
    received = received.astype(jnp.float32)
    groups, _, tokens = meta_ref.shape
    micros = meta_ref.shape[1] // 4
    rows = places_ref.shape[1]
    earlier = lax.broadcasted_iota(jnp.int32, (tokens, tokens), 0) < lax.broadcasted_iota(
        jnp.int32, (tokens, tokens), 1
    )
    earlier = earlier.astype(jnp.bfloat16)
    row = lax.broadcasted_iota(jnp.int32, (rows, tokens), 0)
    weights = []
    for micro in range(micros):
        for j in range(groups):
            meta = meta_ref[j]
            first = meta[4 * micro : 4 * micro + 1] == expert.astype(jnp.float32)
            second = meta[4 * micro + 1 : 4 * micro + 2] == expert.astype(jnp.float32)
            here = jnp.logical_or(first, second)
            weights.append(
                jnp.where(
                    first, meta[4 * micro + 2 : 4 * micro + 3], meta[4 * micro + 3 : 4 * micro + 4]
                )
            )
            named = jnp.broadcast_to(here.astype(jnp.float32), (16, tokens)).astype(jnp.bfloat16)
            slot = jnp.dot(named, earlier, preferred_element_type=jnp.float32)[0:1]
            target = slot.astype(jnp.int32) * groups + (expert ^ j)
            picked = row == jnp.where(here, target, -1)
            places_ref[micro, :, j * tokens : (j + 1) * tokens] = picked.astype(
                jnp.float32
            ).astype(jnp.bfloat16)
    weights = jnp.concatenate(weights, 0)
    padding = jnp.zeros((tokens - weights.shape[0], tokens), jnp.float32)
    weights_ref[...] = jnp.transpose(jnp.concatenate([weights * received, padding], 0))
    kept_ref[...] = jnp.zeros_like(kept_ref) + received


def find_places(meta, cap):
    groups, quads, tokens = meta.shape
    micros = quads // 4
    in_vmem = pl.BlockSpec(memory_space=pltpu.VMEM)
    return pl.pallas_call(
        place_kernel,
        in_specs=[in_vmem],
        out_specs=[in_vmem] * 3,
        out_shape=[
            jax.ShapeDtypeStruct((micros, cap * groups, groups * tokens), jnp.bfloat16),
            jax.ShapeDtypeStruct((tokens, tokens), jnp.float32),
            jax.ShapeDtypeStruct((micros, tokens), jnp.float32),
        ],
        compiler_params=pltpu.CompilerParams(vmem_limit_bytes=16 * MEBI),
    )(meta)


def fill(cut, places_ref, weights_ref, sources, spots, rows_ref):
    micros, rows, _ = places_ref.shape
    tokens, count = weights_ref.shape[0], len(sources[0])
    late = micros * tokens - cut
    for micro in range(micros):
        blocks = []
        for j in range(2 * count):
            top = j // count
            low, high = micro * tokens, (micro + 1) * tokens
            pieces = []
            if low < cut:
                source, at = spots[top]
                pieces.append(sources[source][j % count][at + low : at + min(high, cut), :])
            if high > cut:
                source, at = spots[2]
                at += top * late - cut
                pieces.append(sources[source][j % count][at + max(low, cut) : at + high, :])
            held = pieces[0] if len(pieces) == 1 else jnp.concatenate(pieces, 0)
            weight = weights_ref[:, micro * 2 * count + j : micro * 2 * count + j + 1]
            blocks.append((held.astype(jnp.float32) * weight).astype(jnp.bfloat16))
        rows_ref[micro * rows : (micro + 1) * rows, :] = jnp.dot(
            places_ref[micro], jnp.concatenate(blocks, 0), preferred_element_type=jnp.float32
        ).astype(jnp.bfloat16)


def fill_kernel(cut, count, places_ref, weights_ref, *refs):
    spots = ((0, 0), (0, cut), (0, 2 * cut))
    fill(cut, places_ref, weights_ref, [refs[:count]], spots, refs[-1])


def fill_rows(places, weights, tokens, cut, gates):
    micros, rows, _ = places.shape
    depth = tokens[0].shape[1]
    in_vmem = pl.BlockSpec(memory_space=pltpu.VMEM)
    return pl.pallas_call(
        functools.partial(fill_kernel, cut, len(tokens)),
        in_specs=[in_vmem] * (2 + len(tokens))
        + [pl.BlockSpec(memory_space=pl.ANY)] * len(gates),
        out_specs=in_vmem,
        out_shape=jax.ShapeDtypeStruct((micros * rows, depth), jnp.bfloat16),
        compiler_params=pltpu.CompilerParams(vmem_limit_bytes=12 * MEBI),
    )(places, weights, *tokens, *gates)


def receives():
    return lax.axis_index("pipe") < lax.axis_size("pipe") - 1


def column_copies(weights_hbm, which, held_ref, done):
    hidden, depth = held_ref.shape
    together = depth * lax.axis_size("dp") // weights_hbm.shape[2]
    share = (lax.axis_index("dp") // together) ^ which
    block = hidden // done.shape[0]
    columns = pl.ds(pl.multiple_of(share * depth, 128), depth)
    return [
        pltpu.make_async_copy(
            weights_hbm.at[0, pl.ds(i * block, block), columns],
            held_ref.at[pl.ds(i * block, block), :],
            done.at[i],
        )
        for i in range(done.shape[0])
    ]


def fetch_kernel(which, weights_hbm, *refs):
    held_ref, done = refs[-2:]

    @pl.when(receives())
    def _():
        copies = column_copies(weights_hbm, which, held_ref, done)
        for copy in copies:
            copy.start()
        for copy in copies:
            copy.wait()


def fetch(which, weights, depth, gates):
    return pl.pallas_call(
        functools.partial(fetch_kernel, which),
        in_specs=[pl.BlockSpec(memory_space=pltpu.HBM)]
        + [pl.BlockSpec(memory_space=pl.ANY)] * len(gates),
        out_specs=pl.BlockSpec(memory_space=pltpu.VMEM),
        out_shape=jax.ShapeDtypeStruct((weights.shape[1], depth), weights.dtype),
        scratch_shapes=[pltpu.SemaphoreType.DMA((COPIES,))],
        compiler_params=pltpu.CompilerParams(vmem_limit_bytes=1 * MEBI),
    )(pltpu.with_memory_space_constraint(weights, pltpu.HBM), *gates)


def multiply(row_refs, weight_refs, here):
    product = None
    for row_ref, weight_ref in zip(row_refs, weight_refs):
        term = lax.dot_general(
            row_ref[...], weight_ref[here, :], NT, preferred_element_type=jnp.float32
        )
        product = term if product is None else product + term
    return product


def first_kernel(block, count, following, weights_hbm, *refs):
    row_refs, weight_refs, rest = refs[:count], refs[count : 2 * count], refs[2 * count :]
    total_ref, token_ref, later_refs, done = rest[0], rest[1], rest[2:-1], rest[-1]
    token_ref[...] = jnp.zeros_like(token_ref)

    @pl.when(receives())
    def _():
        copies = []
        for i, later_ref in enumerate(later_refs):
            copies += column_copies(weights_hbm, following[i], later_ref, done.at[i])
        for copy in copies:
            copy.start()

        @pl.loop(0, total_ref.shape[1] // block)
        def _(step):
            here = pl.ds(pl.multiple_of(step * block, block), block)
            total_ref[:, here] = multiply(row_refs, weight_refs, here)

        for copy in copies:
            copy.wait()


def multiply_first(following, rows, held, weights):
    count, depth = rows[0].shape
    hidden, later = weights.shape[1], len(following)
    in_vmem = pl.BlockSpec(memory_space=pltpu.VMEM)
    outs = pl.pallas_call(
        functools.partial(first_kernel, min(1024, hidden), len(rows), following),
        in_specs=[pl.BlockSpec(memory_space=pltpu.HBM)] + [in_vmem] * (2 * len(rows)),
        out_specs=[in_vmem] * (2 + later),
        out_shape=[
            jax.ShapeDtypeStruct((count, hidden), jnp.float32),
            jax.ShapeDtypeStruct((8, 128), jnp.float32),
        ]
        + [jax.ShapeDtypeStruct((hidden, depth), weights.dtype)] * later,
        scratch_shapes=[pltpu.SemaphoreType.DMA((later, COPIES))],
        compiler_params=pltpu.CompilerParams(vmem_limit_bytes=12 * MEBI),
        cost_estimate=pl.CostEstimate(
            flops=2 * count * depth * len(rows) * hidden,
            bytes_accessed=2 * hidden * depth * len(rows),
            transcendentals=0,
        ),
    )(pltpu.with_memory_space_constraint(weights, pltpu.HBM), *rows, *held)
    return outs[0], outs[1], outs[2:]


def last_kernel(groups, cut, each, spots, places_ref, weights_ref, total_ref, *refs):
    count = len(spots)
    out_ref, row_refs = refs[-1 - count], refs[-count:]
    weight_refs, token_refs = refs[:count], refs[count : -1 - count]
    sources = [token_refs[i : i + each] for i in range(0, len(token_refs), each)]

    @pl.when(jnp.logical_and(pl.program_id(0) == 0, receives()))
    def _():
        for i in range(count):
            fill(cut, places_ref, weights_ref, sources, spots[i], row_refs[i])

    micros, cap, block = out_ref.shape[1], out_ref.shape[3], out_ref.shape[5]
    here = pl.ds(pl.multiple_of(pl.program_id(0) * block, block), block)

    @pl.when(receives())
    def _():
        product = multiply(row_refs, weight_refs, here) + total_ref[:, here]
        rows = cap * groups
        for micro in range(micros):
            out_ref[0, micro, 0] = (
                product[micro * rows : (micro + 1) * rows]
                .astype(out_ref.dtype)
                .reshape(cap, groups, block)
            )

    @pl.when(jnp.logical_not(receives()))
    def _():
        out_ref[...] = jnp.zeros_like(out_ref)


def multiply_last(places, weights, tokens, spots, held, total, groups, cut):
    micros = places.shape[0]
    count, hidden = total.shape
    depth = held[0].shape[1]
    block = min(1024, hidden)
    cap = count // (micros * groups)
    in_vmem = pl.BlockSpec(memory_space=pltpu.VMEM)
    args = [places, weights, total, *held, *[ref for refs in tokens for ref in refs]]
    return pl.pallas_call(
        functools.partial(last_kernel, groups, cut, len(tokens[0]), spots),
        grid=(hidden // block,),
        in_specs=[in_vmem] * len(args),
        out_specs=pl.BlockSpec((1, micros, 1, cap, groups, block), lambda f: (0, 0, 0, 0, 0, f)),
        out_shape=jax.ShapeDtypeStruct((1, micros, 1, cap, groups, hidden), jnp.bfloat16),
        scratch_shapes=[pltpu.VMEM((count, depth), jnp.bfloat16)] * len(held),
        compiler_params=pltpu.CompilerParams(vmem_limit_bytes=20 * MEBI),
        cost_estimate=pl.CostEstimate(
            flops=2 * count * depth * len(held) * hidden,
            bytes_accessed=2 * hidden * depth * len(held),
            transcendentals=0,
        ),
    )(*args)


def per_device(out_grad, expert_outputs, logits, routes, down_weights):
    micros, token_count, share = out_grad.shape[1:]
    experts, shares = lax.axis_size("expert"), lax.axis_size("dp")
    cap = min(token_count, 2 * token_count // experts + token_count // 32)
    mine = lax.axis_index("dp")
    sections = lax.axis_size("pipe")
    together = 1
    while (share * together) % 128:
        together *= 2
    sets = list(range(shares // together))
    half = len(sets) // 2
    if together == 1:
        sets = [2, 0, 1, *sets[3:]]
    top = experts // 2
    cut = micros * token_count * 11 // 16
    own = out_grad.reshape(micros * token_count, share)
    early, late = own[:cut], own[cut:]
    late = from_next(late)
    direct = {2: from_next(early, 2)}
    late_top = swap(late, top)

    extra = extra_rows(
        share,
        [],
        logits[0].transpose(0, 2, 1),
        routes[0].transpose(0, 2, 1),
        out_grad[0],
        expert_outputs[0],
    )
    extras = {}
    direct[0] = from_next(join([early, extra], [late]))
    direct[1] = from_next(join([early, extra], [direct[0]]), 1)
    pair = join([late, late_top])
    pairs = {0: pair, 2: from_share(pair, 2, sections - 1), 1: from_share(pair, 1, sections - 1)}
    for k in range(3, shares):
        direct[k] = from_next(join([early, extra], [direct[k - 1]]), k)
        pairs[k] = from_share(join([pair], [pairs[k - 2]]), k, sections - 1)
    near = from_next(join([extra], [direct[shares - 1]]), 2)
    extras[0] = direct[0][cut:]
    direct_top = {0: swap(direct[0], top)[:cut]}
    early_top = swap(join([direct[2], extras[0]]), top)
    direct_top[2], extra_top = early_top[:cut], early_top[cut:]
    for k in range(shares):
        if k != 2:
            direct[k], extras[k] = direct[k][:cut], direct[k][cut:]
        if k and k != 2:
            direct_top[k] = swap(direct[k], top)

    def spread(x):
        held, bit = {0: x}, top // 2
        while bit:
            for j in sorted(held):
                held[j ^ bit] = swap(held[j], bit)
            bit //= 2
        return [held[j] for j in sorted(held)]

    metas = spread(jnp.stack([x[:, :token_count] for x in (extras[0], extra_top)]))
    metas = jnp.concatenate([jnp.stack([m[b] for m in metas]) for b in range(2)], 0)
    metas = metas.astype(jnp.float32).reshape(experts, micros, 8, token_count)
    gap = metas[:, :, 2] + metas[:, :, 3] + metas[:, :, 4]
    weight_first, weight_second = jax.nn.sigmoid(gap), jax.nn.sigmoid(-gap)
    meta = jnp.stack(
        [
            metas[:, :, 0],
            metas[:, :, 1],
            weight_first,
            weight_second,
        ],
        2,
    ).reshape(experts, 4 * micros, token_count)

    places, weights, kept = find_places(meta, cap)
    def gather(which, gates):
        pieces = []
        for k in range(which * together, (which + 1) * together):
            pieces.append(spread(join([direct[k], direct_top[k], pairs[k]], gates)))
        tokens = pieces[0]
        if together > 1:
            order = jnp.arange(together) ^ (mine % together)
            tokens = []
            for j in range(top):
                stacked = jnp.take(jnp.stack([piece[j] for piece in pieces]), order, axis=0)
                tokens.append(stacked.transpose(1, 0, 2).reshape(-1, together * share))
        return tokens

    fetch_gates = [[pairs[2]], [pairs[2]]]
    held = []
    for i in range(half):
        gates = fetch_gates[i] if i < len(fetch_gates) else []
        held.append(fetch(sets[i], down_weights, together * share, gates))
    gates = []
    if together == 1:
        one, three = sets[half:]
        ahead = spread(join([direct[one], pairs[one], direct[three]]))
        gates = []
    rows = [fill_rows(places, weights, gather(which, []), cut, gates) for which in sets[:half]]
    total, done, held = multiply_first(sets[half:], rows, held, down_weights)
    extras[2] = join([near], [done])
    scores = 0.0
    for k in range(shares):
        terms = extras[k][:, :token_count].astype(jnp.float32).reshape(micros, 8, token_count)
        scores += terms[:, 5] + terms[:, 6] + terms[:, 7]
    slope = jnp.where(kept > 0, weight_first[0] * weight_second[0] * scores, 0.0)
    moved_logits = jnp.stack([slope, -slope], -1).astype(jnp.bfloat16)[None]

    if together > 1:
        tokens = [gather(which, [done]) for which in sets[half:]]
        spots = [((i, 0), (i, cut), (i, 2 * cut)) for i in range(len(tokens))]
    else:
        rest = join([direct_top[one], direct_top[three], pairs[three]], [done])
        tokens, both = [ahead, spread(rest)], 2 * (micros * token_count - cut)
        spots = [((0, 0), (1, 0), (0, cut)), ((0, cut + both), (1, cut), (1, 2 * cut))]
    hidden = multiply_last(places, weights, tokens, spots, held, total, experts, cut)
    return hidden.transpose(0, 1, 2, 4, 3, 5), moved_logits


def solution(mesh):
    in_specs = (
        P("pipe", None, "expert", "dp"),
        P("pipe", None, "expert", None, "dp"),
        P("pipe", None, "expert", None),
        P("pipe", None, "expert", None),
        P("expert", "dp", None),
    )
    out_specs = (P("pipe", None, "expert", None, None, "dp"), P("pipe", None, "expert", None))
    return jax.shard_map(
        per_device, mesh=mesh, in_specs=in_specs, out_specs=out_specs, check_vma=False
    )
```

```python
import functools

import jax
import jax.numpy as jnp
from jax import lax
from jax.experimental import pallas as pl
from jax.experimental.pallas import tpu as pltpu
from jax.sharding import PartitionSpec as P

MEBI = 1024 * 1024
NT = (((1,), (1,)), ((), ()))
EXTRA = 16
COPIES = 4


def from_next(x, dp_xor=0):
    sections, shares = lax.axis_size("pipe"), lax.axis_size("dp")
    pairs = [
        (s * shares + z, (s - 1) * shares + (z ^ dp_xor))
        if s
        else (z, (sections - 1) * shares + z)
        for s in range(sections)
        for z in range(shares)
    ]
    return lax.ppermute(x, ("pipe", "dp"), pairs)


def from_share(x, dp_xor, idle):
    sections, shares = lax.axis_size("pipe"), lax.axis_size("dp")
    experts = lax.axis_size("expert")
    pairs = []
    for s in range(sections):
        for z in range(shares):
            for e in range(experts):
                to = (s, z, e ^ 1) if s == idle else (s, z ^ dp_xor, e)
                pairs.append(
                    ((s * shares + z) * experts + e, (to[0] * shares + to[1]) * experts + to[2])
                )
    return lax.ppermute(x, ("pipe", "dp", "expert"), pairs)


def swap(x, bit):
    experts = lax.axis_size("expert")
    return lax.ppermute(x, "expert", [(e, e ^ bit) for e in range(experts)])


def join_kernel(count, *refs):
    out_ref, at = refs[-1], 0
    for ref in refs[:count]:
        out_ref[at : at + ref.shape[0], :] = ref[...]
        at += ref.shape[0]


def join(blocks, gates=()):
    blocks, gates = list(blocks), [gate for gate in gates if gate is not None]
    rows, share = sum(block.shape[0] for block in blocks), blocks[0].shape[1]
    return pl.pallas_call(
        functools.partial(join_kernel, len(blocks)),
        in_specs=[pl.BlockSpec(memory_space=pltpu.VMEM)] * len(blocks)
        + [pl.BlockSpec(memory_space=pl.ANY)] * len(gates),
        out_specs=pl.BlockSpec(memory_space=pltpu.VMEM),
        out_shape=jax.ShapeDtypeStruct((rows, share), blocks[0].dtype),
        compiler_params=pltpu.CompilerParams(vmem_limit_bytes=4 * MEBI),
    )(*blocks, *gates)


def thirds(x):
    high = x.astype(jnp.bfloat16).astype(jnp.float32)
    middle = (x - high).astype(jnp.bfloat16).astype(jnp.float32)
    return [high, middle, x - high - middle]


def extra_kernel(*refs):
    extra_ref, held, done = refs[-6], refs[-5:-1], refs[-1]
    copies = [pltpu.make_async_copy(refs[i], held[i], done.at[i]) for i in range(4)]
    for copy in copies:
        copy.start()
    for copy in copies:
        copy.wait()
    logits_ref, routes_ref, grads_ref, outputs_ref = held
    micros, _, tokens = logits_ref.shape
    share = extra_ref.shape[1]
    pair = lax.broadcasted_iota(jnp.int32, (2 * tokens, tokens), 0)
    token = lax.broadcasted_iota(jnp.int32, (2 * tokens, tokens), 1)
    lines = []
    for micro in range(micros):
        routes = routes_ref[micro].astype(jnp.float32)
        gap = logits_ref[micro, 0:1] - logits_ref[micro, 1:2]
        products = lax.dot_general(
            outputs_ref[micro].reshape(2 * tokens, share),
            grads_ref[micro],
            NT,
            preferred_element_type=jnp.float32,
        )
        first = jnp.sum(jnp.where(pair == 2 * token, products, 0.0), 0, keepdims=True)
        second = jnp.sum(jnp.where(pair == 2 * token + 1, products, 0.0), 0, keepdims=True)
        lines += [routes[0:1], routes[1:2], *thirds(gap), *thirds(first - second)]
    lines = jnp.concatenate(lines, 0)
    if share > tokens:
        lines = jnp.concatenate([lines, jnp.zeros((EXTRA, share - tokens), jnp.float32)], 1)
    extra_ref[...] = lines.astype(jnp.bfloat16)


def extra_rows(share, gates, *args):
    return pl.pallas_call(
        extra_kernel,
        in_specs=[pl.BlockSpec(memory_space=pltpu.HBM)] * len(args)
        + [pl.BlockSpec(memory_space=pl.ANY)] * len(gates),
        out_specs=pl.BlockSpec(memory_space=pltpu.VMEM),
        out_shape=jax.ShapeDtypeStruct((EXTRA, share), jnp.bfloat16),
        scratch_shapes=[pltpu.VMEM(arg.shape, arg.dtype) for arg in args]
        + [pltpu.SemaphoreType.DMA((len(args),))],
        compiler_params=pltpu.CompilerParams(vmem_limit_bytes=4 * MEBI),
    )(*[pltpu.with_memory_space_constraint(arg, pltpu.HBM) for arg in args], *gates)


def place_kernel(meta_ref, places_ref, weights_ref, kept_ref):
    expert = lax.axis_index("expert")
    received = lax.axis_index("pipe") < lax.axis_size("pipe") - 1
    received = received.astype(jnp.float32)
    groups, _, tokens = meta_ref.shape
    micros = meta_ref.shape[1] // 4
    rows = places_ref.shape[1]
    earlier = lax.broadcasted_iota(jnp.int32, (tokens, tokens), 0) < lax.broadcasted_iota(
        jnp.int32, (tokens, tokens), 1
    )
    earlier = earlier.astype(jnp.bfloat16)
    row = lax.broadcasted_iota(jnp.int32, (rows, tokens), 0)
    weights = []
    for micro in range(micros):
        for j in range(groups):
            meta = meta_ref[j]
            first = meta[4 * micro : 4 * micro + 1] == expert.astype(jnp.float32)
            second = meta[4 * micro + 1 : 4 * micro + 2] == expert.astype(jnp.float32)
            here = jnp.logical_or(first, second)
            weights.append(
                jnp.where(
                    first, meta[4 * micro + 2 : 4 * micro + 3], meta[4 * micro + 3 : 4 * micro + 4]
                )
            )
            named = jnp.broadcast_to(here.astype(jnp.float32), (16, tokens)).astype(jnp.bfloat16)
            slot = jnp.dot(named, earlier, preferred_element_type=jnp.float32)[0:1]
            target = slot.astype(jnp.int32) * groups + (expert ^ j)
            picked = row == jnp.where(here, target, -1)
            places_ref[micro, :, j * tokens : (j + 1) * tokens] = picked.astype(
                jnp.float32
            ).astype(jnp.bfloat16)
    weights = jnp.concatenate(weights, 0)
    padding = jnp.zeros((tokens - weights.shape[0], tokens), jnp.float32)
    weights_ref[...] = jnp.transpose(jnp.concatenate([weights * received, padding], 0))
    kept_ref[...] = jnp.zeros_like(kept_ref) + received


def find_places(meta, cap):
    groups, quads, tokens = meta.shape
    micros = quads // 4
    in_vmem = pl.BlockSpec(memory_space=pltpu.VMEM)
    return pl.pallas_call(
        place_kernel,
        in_specs=[in_vmem],
        out_specs=[in_vmem] * 3,
        out_shape=[
            jax.ShapeDtypeStruct((micros, cap * groups, groups * tokens), jnp.bfloat16),
            jax.ShapeDtypeStruct((tokens, tokens), jnp.float32),
            jax.ShapeDtypeStruct((micros, tokens), jnp.float32),
        ],
        compiler_params=pltpu.CompilerParams(vmem_limit_bytes=16 * MEBI),
    )(meta)


def fill(cut, places_ref, weights_ref, sources, spots, rows_ref):
    micros, rows, _ = places_ref.shape
    tokens, count = weights_ref.shape[0], len(sources[0])
    late = micros * tokens - cut
    for micro in range(micros):
        blocks = []
        for j in range(2 * count):
            top = j // count
            low, high = micro * tokens, (micro + 1) * tokens
            pieces = []
            if low < cut:
                source, at = spots[top]
                pieces.append(sources[source][j % count][at + low : at + min(high, cut), :])
            if high > cut:
                source, at = spots[2]
                at += top * late - cut
                pieces.append(sources[source][j % count][at + max(low, cut) : at + high, :])
            held = pieces[0] if len(pieces) == 1 else jnp.concatenate(pieces, 0)
            weight = weights_ref[:, micro * 2 * count + j : micro * 2 * count + j + 1]
            blocks.append((held.astype(jnp.float32) * weight).astype(jnp.bfloat16))
        rows_ref[micro * rows : (micro + 1) * rows, :] = jnp.dot(
            places_ref[micro], jnp.concatenate(blocks, 0), preferred_element_type=jnp.float32
        ).astype(jnp.bfloat16)


def fill_kernel(cut, count, places_ref, weights_ref, *refs):
    spots = ((0, 0), (0, cut), (0, 2 * cut))
    fill(cut, places_ref, weights_ref, [refs[:count]], spots, refs[-1])


def fill_rows(places, weights, tokens, cut, gates):
    micros, rows, _ = places.shape
    depth = tokens[0].shape[1]
    in_vmem = pl.BlockSpec(memory_space=pltpu.VMEM)
    return pl.pallas_call(
        functools.partial(fill_kernel, cut, len(tokens)),
        in_specs=[in_vmem] * (2 + len(tokens))
        + [pl.BlockSpec(memory_space=pl.ANY)] * len(gates),
        out_specs=in_vmem,
        out_shape=jax.ShapeDtypeStruct((micros * rows, depth), jnp.bfloat16),
        compiler_params=pltpu.CompilerParams(vmem_limit_bytes=12 * MEBI),
    )(places, weights, *tokens, *gates)


def receives():
    return lax.axis_index("pipe") < lax.axis_size("pipe") - 1


def column_copies(weights_hbm, which, held_ref, done):
    hidden, depth = held_ref.shape
    together = depth * lax.axis_size("dp") // weights_hbm.shape[2]
    share = (lax.axis_index("dp") // together) ^ which
    block = hidden // done.shape[0]
    columns = pl.ds(pl.multiple_of(share * depth, 128), depth)
    return [
        pltpu.make_async_copy(
            weights_hbm.at[0, pl.ds(i * block, block), columns],
            held_ref.at[pl.ds(i * block, block), :],
            done.at[i],
        )
        for i in range(done.shape[0])
    ]


def fetch_kernel(which, weights_hbm, *refs):
    held_ref, done = refs[-2:]

    @pl.when(receives())
    def _():
        copies = column_copies(weights_hbm, which, held_ref, done)
        for copy in copies:
            copy.start()
        for copy in copies:
            copy.wait()


def fetch(which, weights, depth, gates):
    return pl.pallas_call(
        functools.partial(fetch_kernel, which),
        in_specs=[pl.BlockSpec(memory_space=pltpu.HBM)]
        + [pl.BlockSpec(memory_space=pl.ANY)] * len(gates),
        out_specs=pl.BlockSpec(memory_space=pltpu.VMEM),
        out_shape=jax.ShapeDtypeStruct((weights.shape[1], depth), weights.dtype),
        scratch_shapes=[pltpu.SemaphoreType.DMA((COPIES,))],
        compiler_params=pltpu.CompilerParams(vmem_limit_bytes=1 * MEBI),
    )(pltpu.with_memory_space_constraint(weights, pltpu.HBM), *gates)


def multiply(row_refs, weight_refs, here):
    product = None
    for row_ref, weight_ref in zip(row_refs, weight_refs):
        term = lax.dot_general(
            row_ref[...], weight_ref[here, :], NT, preferred_element_type=jnp.float32
        )
        product = term if product is None else product + term
    return product


def first_kernel(block, count, following, weights_hbm, *refs):
    row_refs, weight_refs, rest = refs[:count], refs[count : 2 * count], refs[2 * count :]
    total_ref, token_ref, later_refs, done = rest[0], rest[1], rest[2:-1], rest[-1]
    token_ref[...] = jnp.zeros_like(token_ref)

    @pl.when(receives())
    def _():
        copies = []
        for i, later_ref in enumerate(later_refs):
            copies += column_copies(weights_hbm, following[i], later_ref, done.at[i])
        for copy in copies:
            copy.start()

        @pl.loop(0, total_ref.shape[1] // block)
        def _(step):
            here = pl.ds(pl.multiple_of(step * block, block), block)
            total_ref[:, here] = multiply(row_refs, weight_refs, here)

        for copy in copies:
            copy.wait()


def multiply_first(following, rows, held, weights):
    count, depth = rows[0].shape
    hidden, later = weights.shape[1], len(following)
    in_vmem = pl.BlockSpec(memory_space=pltpu.VMEM)
    outs = pl.pallas_call(
        functools.partial(first_kernel, min(1024, hidden), len(rows), following),
        in_specs=[pl.BlockSpec(memory_space=pltpu.HBM)] + [in_vmem] * (2 * len(rows)),
        out_specs=[in_vmem] * (2 + later),
        out_shape=[
            jax.ShapeDtypeStruct((count, hidden), jnp.float32),
            jax.ShapeDtypeStruct((8, 128), jnp.float32),
        ]
        + [jax.ShapeDtypeStruct((hidden, depth), weights.dtype)] * later,
        scratch_shapes=[pltpu.SemaphoreType.DMA((later, COPIES))],
        compiler_params=pltpu.CompilerParams(vmem_limit_bytes=12 * MEBI),
        cost_estimate=pl.CostEstimate(flops=1, bytes_accessed=1, transcendentals=0),
    )(pltpu.with_memory_space_constraint(weights, pltpu.HBM), *rows, *held)
    return outs[0], outs[1], outs[2:]


def last_kernel(groups, cut, each, spots, places_ref, weights_ref, total_ref, *refs):
    count = len(spots)
    out_ref, row_refs = refs[-1 - count], refs[-count:]
    weight_refs, token_refs = refs[:count], refs[count : -1 - count]
    sources = [token_refs[i : i + each] for i in range(0, len(token_refs), each)]

    @pl.when(jnp.logical_and(pl.program_id(0) == 0, receives()))
    def _():
        for i in range(count):
            fill(cut, places_ref, weights_ref, sources, spots[i], row_refs[i])

    micros, cap, block = out_ref.shape[1], out_ref.shape[3], out_ref.shape[5]
    here = pl.ds(pl.multiple_of(pl.program_id(0) * block, block), block)

    @pl.when(receives())
    def _():
        product = multiply(row_refs, weight_refs, here) + total_ref[:, here]
        rows = cap * groups
        for micro in range(micros):
            out_ref[0, micro, 0] = (
                product[micro * rows : (micro + 1) * rows]
                .astype(out_ref.dtype)
                .reshape(cap, groups, block)
            )

    @pl.when(jnp.logical_not(receives()))
    def _():
        out_ref[...] = jnp.zeros_like(out_ref)


def multiply_last(places, weights, tokens, spots, held, total, groups, cut):
    micros = places.shape[0]
    count, hidden = total.shape
    depth = held[0].shape[1]
    block = min(1024, hidden)
    cap = count // (micros * groups)
    in_vmem = pl.BlockSpec(memory_space=pltpu.VMEM)
    args = [places, weights, total, *held, *[ref for refs in tokens for ref in refs]]
    return pl.pallas_call(
        functools.partial(last_kernel, groups, cut, len(tokens[0]), spots),
        grid=(hidden // block,),
        in_specs=[in_vmem] * len(args),
        out_specs=pl.BlockSpec((1, micros, 1, cap, groups, block), lambda f: (0, 0, 0, 0, 0, f)),
        out_shape=jax.ShapeDtypeStruct((1, micros, 1, cap, groups, hidden), jnp.bfloat16),
        scratch_shapes=[pltpu.VMEM((count, depth), jnp.bfloat16)] * len(held),
        compiler_params=pltpu.CompilerParams(vmem_limit_bytes=20 * MEBI),
        cost_estimate=pl.CostEstimate(
            flops=2 * count * depth * len(held) * hidden,
            bytes_accessed=2 * hidden * depth * len(held),
            transcendentals=0,
        ),
    )(*args)


def per_device(out_grad, expert_outputs, logits, routes, down_weights):
    micros, token_count, share = out_grad.shape[1:]
    experts, shares = lax.axis_size("expert"), lax.axis_size("dp")
    cap = min(token_count, 2 * token_count // experts + token_count // 32)
    mine = lax.axis_index("dp")
    sections = lax.axis_size("pipe")
    together = 1
    while (share * together) % 128:
        together *= 2
    sets = list(range(shares // together))
    half = len(sets) // 2
    if together == 1:
        sets = [2, 0, 1, *sets[3:]]
    top = experts // 2
    cut = micros * token_count * 11 // 16
    own = out_grad.reshape(micros * token_count, share)
    early, late = own[:cut], own[cut:]
    late = from_next(late)
    direct = {2: from_next(early, 2)}
    late_top = swap(late, top)

    extra = extra_rows(
        share,
        [],
        logits[0].transpose(0, 2, 1),
        routes[0].transpose(0, 2, 1),
        out_grad[0],
        expert_outputs[0],
    )
    extras = {}
    direct[0] = from_next(join([early, extra], [late]))
    direct[1] = from_next(join([early, extra], [direct[0]]), 1)
    pair = join([late, late_top])
    pairs = {0: pair, 2: from_share(pair, 2, sections - 1), 1: from_share(pair, 1, sections - 1)}
    for k in range(3, shares):
        direct[k] = from_next(join([early, extra], [direct[k - 1]]), k)
        pairs[k] = from_share(join([pair], [pairs[k - 2]]), k, sections - 1)
    pairs_near = [
        (s * shares + z, (s - 1) * shares + (z ^ 2)) for s in range(1, sections) for z in range(shares)
    ]
    near = lax.ppermute(join([extra], [direct[0]]), ("pipe", "dp"), pairs_near)
    extras[0] = direct[0][cut:]
    direct_top = {0: swap(direct[0], top)[:cut]}
    early_top = swap(join([direct[2], extras[0]]), top)
    direct_top[2], extra_top = early_top[:cut], early_top[cut:]
    for k in (0, *range(3, shares)):
        direct[k], extras[k] = direct[k][:cut], direct[k][cut:]
        if k:
            direct_top[k] = swap(direct[k], top)

    def spread(x):
        held, bit = {0: x}, top // 2
        while bit:
            for j in sorted(held):
                held[j ^ bit] = swap(held[j], bit)
            bit //= 2
        return [held[j] for j in sorted(held)]

    metas = spread(jnp.stack([x[:, :token_count] for x in (extras[0], extra_top)]))
    metas = jnp.concatenate([jnp.stack([m[b] for m in metas]) for b in range(2)], 0)
    metas = metas.astype(jnp.float32).reshape(experts, micros, 8, token_count)
    gap = metas[:, :, 2] + metas[:, :, 3] + metas[:, :, 4]
    weight_first, weight_second = jax.nn.sigmoid(gap), jax.nn.sigmoid(-gap)
    meta = jnp.stack(
        [
            metas[:, :, 0],
            metas[:, :, 1],
            weight_first,
            weight_second,
        ],
        2,
    ).reshape(experts, 4 * micros, token_count)

    places, weights, kept = find_places(meta, cap)
    last = join([direct[1]], [places])
    direct[1], extras[1] = last[:cut], last[cut:]
    direct_top[1] = swap(direct[1], top)

    def gather(which, gates):
        pieces = []
        for k in range(which * together, (which + 1) * together):
            pieces.append(spread(join([direct[k], direct_top[k], pairs[k]], gates)))
        tokens = pieces[0]
        if together > 1:
            order = jnp.arange(together) ^ (mine % together)
            tokens = []
            for j in range(top):
                stacked = jnp.take(jnp.stack([piece[j] for piece in pieces]), order, axis=0)
                tokens.append(stacked.transpose(1, 0, 2).reshape(-1, together * share))
        return tokens

    fetch_gates = [[pairs[2]], [pairs[2]]]
    held = []
    for i in range(half):
        gates = fetch_gates[i] if i < len(fetch_gates) else []
        held.append(fetch(sets[i], down_weights, together * share, gates))
    gates = []
    if together == 1:
        one, three = sets[half:]
        ahead = spread(join([direct[one], pairs[one], direct[three]]))
        gates = []
    rows = [fill_rows(places, weights, gather(which, []), cut, gates) for which in sets[:half]]
    total, done, held = multiply_first(sets[half:], rows, held, down_weights)
    extras[2] = join([near], [done])
    scores = 0.0
    for k in range(shares):
        terms = extras[k][:, :token_count].astype(jnp.float32).reshape(micros, 8, token_count)
        scores += terms[:, 5] + terms[:, 6] + terms[:, 7]
    slope = jnp.where(kept > 0, weight_first[0] * weight_second[0] * scores, 0.0)
    moved_logits = jnp.stack([slope, -slope], -1).astype(jnp.bfloat16)[None]

    if together > 1:
        tokens = [gather(which, [done]) for which in sets[half:]]
        spots = [((i, 0), (i, cut), (i, 2 * cut)) for i in range(len(tokens))]
    else:
        rest = join([direct_top[one], direct_top[three], pairs[three]], [done])
        tokens, both = [ahead, spread(rest)], 2 * (micros * token_count - cut)
        spots = [((0, 0), (1, 0), (0, cut)), ((0, cut + both), (1, cut), (1, 2 * cut))]
    hidden = multiply_last(places, weights, tokens, spots, held, total, experts, cut)
    return hidden.transpose(0, 1, 2, 4, 3, 5), moved_logits


def solution(mesh):
    in_specs = (
        P("pipe", None, "expert", "dp"),
        P("pipe", None, "expert", None, "dp"),
        P("pipe", None, "expert", None),
        P("pipe", None, "expert", None),
        P("expert", "dp", None),
    )
    out_specs = (P("pipe", None, "expert", None, None, "dp"), P("pipe", None, "expert", None))
    return jax.shard_map(
        per_device, mesh=mesh, in_specs=in_specs, out_specs=out_specs, check_vma=False
    )
```

```python
import functools

import jax
import jax.numpy as jnp
from jax import lax
from jax.experimental import pallas as pl
from jax.experimental.pallas import tpu as pltpu
from jax.sharding import PartitionSpec as P

MEBI = 1024 * 1024
NT = (((1,), (1,)), ((), ()))
EXTRA = 16
COPIES = 4


def from_next(x, dp_xor=0):
    sections, shares = lax.axis_size("pipe"), lax.axis_size("dp")
    pairs = [
        (s * shares + z, (s - 1) * shares + (z ^ dp_xor))
        if s
        else (z, (sections - 1) * shares + z)
        for s in range(sections)
        for z in range(shares)
    ]
    return lax.ppermute(x, ("pipe", "dp"), pairs)


def from_share(x, dp_xor, idle):
    sections, shares = lax.axis_size("pipe"), lax.axis_size("dp")
    experts = lax.axis_size("expert")
    pairs = []
    for s in range(sections):
        for z in range(shares):
            for e in range(experts):
                to = (s, z, e ^ 1) if s == idle else (s, z ^ dp_xor, e)
                pairs.append(
                    ((s * shares + z) * experts + e, (to[0] * shares + to[1]) * experts + to[2])
                )
    return lax.ppermute(x, ("pipe", "dp", "expert"), pairs)


def swap(x, bit):
    experts = lax.axis_size("expert")
    return lax.ppermute(x, "expert", [(e, e ^ bit) for e in range(experts)])


def join_kernel(count, *refs):
    out_ref, at = refs[-1], 0
    for ref in refs[:count]:
        out_ref[at : at + ref.shape[0], :] = ref[...]
        at += ref.shape[0]


def join(blocks, gates=()):
    blocks, gates = list(blocks), [gate for gate in gates if gate is not None]
    rows, share = sum(block.shape[0] for block in blocks), blocks[0].shape[1]
    return pl.pallas_call(
        functools.partial(join_kernel, len(blocks)),
        in_specs=[pl.BlockSpec(memory_space=pltpu.VMEM)] * len(blocks)
        + [pl.BlockSpec(memory_space=pl.ANY)] * len(gates),
        out_specs=pl.BlockSpec(memory_space=pltpu.VMEM),
        out_shape=jax.ShapeDtypeStruct((rows, share), blocks[0].dtype),
        compiler_params=pltpu.CompilerParams(vmem_limit_bytes=4 * MEBI),
    )(*blocks, *gates)


def thirds(x):
    high = x.astype(jnp.bfloat16).astype(jnp.float32)
    middle = (x - high).astype(jnp.bfloat16).astype(jnp.float32)
    return [high, middle, x - high - middle]


def extra_kernel(*refs):
    extra_ref, held, done = refs[-6], refs[-5:-1], refs[-1]
    copies = [pltpu.make_async_copy(refs[i], held[i], done.at[i]) for i in range(4)]
    for copy in copies:
        copy.start()
    for copy in copies:
        copy.wait()
    logits_ref, routes_ref, grads_ref, outputs_ref = held
    micros, _, tokens = logits_ref.shape
    share = extra_ref.shape[1]
    pair = lax.broadcasted_iota(jnp.int32, (2 * tokens, tokens), 0)
    token = lax.broadcasted_iota(jnp.int32, (2 * tokens, tokens), 1)
    lines = []
    for micro in range(micros):
        routes = routes_ref[micro].astype(jnp.float32)
        gap = logits_ref[micro, 0:1] - logits_ref[micro, 1:2]
        products = lax.dot_general(
            outputs_ref[micro].reshape(2 * tokens, share),
            grads_ref[micro],
            NT,
            preferred_element_type=jnp.float32,
        )
        first = jnp.sum(jnp.where(pair == 2 * token, products, 0.0), 0, keepdims=True)
        second = jnp.sum(jnp.where(pair == 2 * token + 1, products, 0.0), 0, keepdims=True)
        lines += [routes[0:1], routes[1:2], *thirds(gap), *thirds(first - second)]
    lines = jnp.concatenate(lines, 0)
    if share > tokens:
        lines = jnp.concatenate([lines, jnp.zeros((EXTRA, share - tokens), jnp.float32)], 1)
    extra_ref[...] = lines.astype(jnp.bfloat16)


def extra_rows(share, gates, *args):
    return pl.pallas_call(
        extra_kernel,
        in_specs=[pl.BlockSpec(memory_space=pltpu.HBM)] * len(args)
        + [pl.BlockSpec(memory_space=pl.ANY)] * len(gates),
        out_specs=pl.BlockSpec(memory_space=pltpu.VMEM),
        out_shape=jax.ShapeDtypeStruct((EXTRA, share), jnp.bfloat16),
        scratch_shapes=[pltpu.VMEM(arg.shape, arg.dtype) for arg in args]
        + [pltpu.SemaphoreType.DMA((len(args),))],
        compiler_params=pltpu.CompilerParams(vmem_limit_bytes=4 * MEBI),
    )(*[pltpu.with_memory_space_constraint(arg, pltpu.HBM) for arg in args], *gates)


def place_kernel(meta_ref, places_ref, weights_ref, kept_ref):
    expert = lax.axis_index("expert")
    received = lax.axis_index("pipe") < lax.axis_size("pipe") - 1
    received = received.astype(jnp.float32)
    groups, _, tokens = meta_ref.shape
    micros = meta_ref.shape[1] // 4
    rows = places_ref.shape[1]
    earlier = lax.broadcasted_iota(jnp.int32, (tokens, tokens), 0) < lax.broadcasted_iota(
        jnp.int32, (tokens, tokens), 1
    )
    earlier = earlier.astype(jnp.bfloat16)
    row = lax.broadcasted_iota(jnp.int32, (rows, tokens), 0)
    weights = []
    for micro in range(micros):
        for j in range(groups):
            meta = meta_ref[j]
            first = meta[4 * micro : 4 * micro + 1] == expert.astype(jnp.float32)
            second = meta[4 * micro + 1 : 4 * micro + 2] == expert.astype(jnp.float32)
            here = jnp.logical_or(first, second)
            weights.append(
                jnp.where(
                    first, meta[4 * micro + 2 : 4 * micro + 3], meta[4 * micro + 3 : 4 * micro + 4]
                )
            )
            named = jnp.broadcast_to(here.astype(jnp.float32), (16, tokens)).astype(jnp.bfloat16)
            slot = jnp.dot(named, earlier, preferred_element_type=jnp.float32)[0:1]
            target = slot.astype(jnp.int32) * groups + (expert ^ j)
            picked = row == jnp.where(here, target, -1)
            places_ref[micro, :, j * tokens : (j + 1) * tokens] = picked.astype(
                jnp.float32
            ).astype(jnp.bfloat16)
    weights = jnp.concatenate(weights, 0)
    padding = jnp.zeros((tokens - weights.shape[0], tokens), jnp.float32)
    weights_ref[...] = jnp.transpose(jnp.concatenate([weights * received, padding], 0))
    kept_ref[...] = jnp.zeros_like(kept_ref) + received


def find_places(meta, cap):
    groups, quads, tokens = meta.shape
    micros = quads // 4
    in_vmem = pl.BlockSpec(memory_space=pltpu.VMEM)
    return pl.pallas_call(
        place_kernel,
        in_specs=[in_vmem],
        out_specs=[in_vmem] * 3,
        out_shape=[
            jax.ShapeDtypeStruct((micros, cap * groups, groups * tokens), jnp.bfloat16),
            jax.ShapeDtypeStruct((tokens, tokens), jnp.float32),
            jax.ShapeDtypeStruct((micros, tokens), jnp.float32),
        ],
        compiler_params=pltpu.CompilerParams(vmem_limit_bytes=16 * MEBI),
    )(meta)


def fill(cut, places_ref, weights_ref, sources, spots, rows_ref):
    micros, rows, _ = places_ref.shape
    tokens, count = weights_ref.shape[0], len(sources[0])
    late = micros * tokens - cut
    for micro in range(micros):
        blocks = []
        for j in range(2 * count):
            top = j // count
            low, high = micro * tokens, (micro + 1) * tokens
            pieces = []
            if low < cut:
                source, at = spots[top]
                pieces.append(sources[source][j % count][at + low : at + min(high, cut), :])
            if high > cut:
                source, at = spots[2]
                at += top * late - cut
                pieces.append(sources[source][j % count][at + max(low, cut) : at + high, :])
            held = pieces[0] if len(pieces) == 1 else jnp.concatenate(pieces, 0)
            weight = weights_ref[:, micro * 2 * count + j : micro * 2 * count + j + 1]
            blocks.append((held.astype(jnp.float32) * weight).astype(jnp.bfloat16))
        rows_ref[micro * rows : (micro + 1) * rows, :] = jnp.dot(
            places_ref[micro], jnp.concatenate(blocks, 0), preferred_element_type=jnp.float32
        ).astype(jnp.bfloat16)


def fill_kernel(cut, count, places_ref, weights_ref, *refs):
    spots = ((0, 0), (0, cut), (0, 2 * cut))
    fill(cut, places_ref, weights_ref, [refs[:count]], spots, refs[-1])


def fill_rows(places, weights, tokens, cut, gates):
    micros, rows, _ = places.shape
    depth = tokens[0].shape[1]
    in_vmem = pl.BlockSpec(memory_space=pltpu.VMEM)
    return pl.pallas_call(
        functools.partial(fill_kernel, cut, len(tokens)),
        in_specs=[in_vmem] * (2 + len(tokens))
        + [pl.BlockSpec(memory_space=pl.ANY)] * len(gates),
        out_specs=in_vmem,
        out_shape=jax.ShapeDtypeStruct((micros * rows, depth), jnp.bfloat16),
        compiler_params=pltpu.CompilerParams(vmem_limit_bytes=12 * MEBI),
    )(places, weights, *tokens, *gates)


def receives():
    return lax.axis_index("pipe") < lax.axis_size("pipe") - 1


def column_copies(weights_hbm, which, held_ref, done):
    hidden, depth = held_ref.shape
    together = depth * lax.axis_size("dp") // weights_hbm.shape[2]
    share = (lax.axis_index("dp") // together) ^ which
    block = hidden // done.shape[0]
    columns = pl.ds(pl.multiple_of(share * depth, 128), depth)
    return [
        pltpu.make_async_copy(
            weights_hbm.at[0, pl.ds(i * block, block), columns],
            held_ref.at[pl.ds(i * block, block), :],
            done.at[i],
        )
        for i in range(done.shape[0])
    ]


def fetch_kernel(which, weights_hbm, *refs):
    held_ref, done = refs[-2:]

    @pl.when(receives())
    def _():
        copies = column_copies(weights_hbm, which, held_ref, done)
        for copy in copies:
            copy.start()
        for copy in copies:
            copy.wait()


def fetch(which, weights, depth, gates):
    return pl.pallas_call(
        functools.partial(fetch_kernel, which),
        in_specs=[pl.BlockSpec(memory_space=pltpu.HBM)]
        + [pl.BlockSpec(memory_space=pl.ANY)] * len(gates),
        out_specs=pl.BlockSpec(memory_space=pltpu.VMEM),
        out_shape=jax.ShapeDtypeStruct((weights.shape[1], depth), weights.dtype),
        scratch_shapes=[pltpu.SemaphoreType.DMA((COPIES,))],
        compiler_params=pltpu.CompilerParams(vmem_limit_bytes=1 * MEBI),
    )(pltpu.with_memory_space_constraint(weights, pltpu.HBM), *gates)


def multiply(row_refs, weight_refs, here):
    product = None
    for row_ref, weight_ref in zip(row_refs, weight_refs):
        term = lax.dot_general(
            row_ref[...], weight_ref[here, :], NT, preferred_element_type=jnp.float32
        )
        product = term if product is None else product + term
    return product


def first_kernel(block, count, following, weights_hbm, *refs):
    row_refs, weight_refs, rest = refs[:count], refs[count : 2 * count], refs[2 * count :]
    total_ref, token_ref, later_refs, done = rest[0], rest[1], rest[2:-1], rest[-1]
    token_ref[...] = jnp.zeros_like(token_ref)

    @pl.when(receives())
    def _():
        copies = []
        for i, later_ref in enumerate(later_refs):
            copies += column_copies(weights_hbm, following[i], later_ref, done.at[i])
        for copy in copies:
            copy.start()

        @pl.loop(0, total_ref.shape[1] // block)
        def _(step):
            here = pl.ds(pl.multiple_of(step * block, block), block)
            total_ref[:, here] = multiply(row_refs, weight_refs, here)

        for copy in copies:
            copy.wait()


def multiply_first(following, rows, held, weights):
    count, depth = rows[0].shape
    hidden, later = weights.shape[1], len(following)
    in_vmem = pl.BlockSpec(memory_space=pltpu.VMEM)
    outs = pl.pallas_call(
        functools.partial(first_kernel, min(1024, hidden), len(rows), following),
        in_specs=[pl.BlockSpec(memory_space=pltpu.HBM)] + [in_vmem] * (2 * len(rows)),
        out_specs=[in_vmem] * (2 + later),
        out_shape=[
            jax.ShapeDtypeStruct((count, hidden), jnp.float32),
            jax.ShapeDtypeStruct((8, 128), jnp.float32),
        ]
        + [jax.ShapeDtypeStruct((hidden, depth), weights.dtype)] * later,
        scratch_shapes=[pltpu.SemaphoreType.DMA((later, COPIES))],
        compiler_params=pltpu.CompilerParams(vmem_limit_bytes=12 * MEBI),
        cost_estimate=pl.CostEstimate(flops=1, bytes_accessed=1, transcendentals=0),
    )(pltpu.with_memory_space_constraint(weights, pltpu.HBM), *rows, *held)
    return outs[0], outs[1], outs[2:]


def last_kernel(groups, cut, each, spots, places_ref, weights_ref, total_ref, *refs):
    count = len(spots)
    out_ref, row_refs = refs[-1 - count], refs[-count:]
    weight_refs, token_refs = refs[:count], refs[count : -1 - count]
    sources = [token_refs[i : i + each] for i in range(0, len(token_refs), each)]

    @pl.when(jnp.logical_and(pl.program_id(0) == 0, receives()))
    def _():
        for i in range(count):
            fill(cut, places_ref, weights_ref, sources, spots[i], row_refs[i])

    micros, cap, block = out_ref.shape[1], out_ref.shape[3], out_ref.shape[5]
    here = pl.ds(pl.multiple_of(pl.program_id(0) * block, block), block)

    @pl.when(receives())
    def _():
        product = multiply(row_refs, weight_refs, here) + total_ref[:, here]
        rows = cap * groups
        for micro in range(micros):
            out_ref[0, micro, 0] = (
                product[micro * rows : (micro + 1) * rows]
                .astype(out_ref.dtype)
                .reshape(cap, groups, block)
            )

    @pl.when(jnp.logical_not(receives()))
    def _():
        out_ref[...] = jnp.zeros_like(out_ref)


def multiply_last(places, weights, tokens, spots, held, total, groups, cut):
    micros = places.shape[0]
    count, hidden = total.shape
    depth = held[0].shape[1]
    block = min(1024, hidden)
    cap = count // (micros * groups)
    in_vmem = pl.BlockSpec(memory_space=pltpu.VMEM)
    args = [places, weights, total, *held, *[ref for refs in tokens for ref in refs]]
    return pl.pallas_call(
        functools.partial(last_kernel, groups, cut, len(tokens[0]), spots),
        grid=(hidden // block,),
        in_specs=[in_vmem] * len(args),
        out_specs=pl.BlockSpec((1, micros, 1, cap, groups, block), lambda f: (0, 0, 0, 0, 0, f)),
        out_shape=jax.ShapeDtypeStruct((1, micros, 1, cap, groups, hidden), jnp.bfloat16),
        scratch_shapes=[pltpu.VMEM((count, depth), jnp.bfloat16)] * len(held),
        compiler_params=pltpu.CompilerParams(vmem_limit_bytes=20 * MEBI),
        cost_estimate=pl.CostEstimate(
            flops=2 * count * depth * len(held) * hidden,
            bytes_accessed=2 * hidden * depth * len(held),
            transcendentals=0,
        ),
    )(*args)


def per_device(out_grad, expert_outputs, logits, routes, down_weights):
    micros, token_count, share = out_grad.shape[1:]
    experts, shares = lax.axis_size("expert"), lax.axis_size("dp")
    cap = min(token_count, 2 * token_count // experts + token_count // 32)
    mine = lax.axis_index("dp")
    sections = lax.axis_size("pipe")
    together = 1
    while (share * together) % 128:
        together *= 2
    sets = list(range(shares // together))
    half = len(sets) // 2
    if together == 1:
        sets = [2, 0, 1, *sets[3:]]
    top = experts // 2
    cut = micros * token_count * 11 // 16
    own = out_grad.reshape(micros * token_count, share)
    early, late = own[:cut], own[cut:]
    late = from_next(late)
    direct = {2: from_next(early, 2)}
    late_top = swap(late, top)

    extra = extra_rows(
        share,
        [],
        logits[0].transpose(0, 2, 1),
        routes[0].transpose(0, 2, 1),
        out_grad[0],
        expert_outputs[0],
    )
    extras = {}
    direct[0] = from_next(join([early, extra], [late]))
    direct[1] = from_next(join([early, extra], [direct[0]]), 1)
    pair = join([late, late_top])
    pairs = {0: pair, 2: from_share(pair, 2, sections - 1), 1: from_share(pair, 1, sections - 1)}
    for k in range(3, shares):
        direct[k] = from_next(join([early, extra], [direct[k - 1]]), k)
        pairs[k] = from_share(join([pair], [pairs[k - 2]]), k, sections - 1)
    pairs_near = [
        (s * shares + z, (s - 1) * shares + (z ^ 2)) for s in range(1, sections) for z in range(shares)
    ]
    near = lax.ppermute(join([extra], [direct[0]]), ("pipe", "dp"), pairs_near)
    extras[0] = direct[0][cut:]
    direct_top = {0: swap(direct[0], top)[:cut]}
    early_top = swap(join([direct[2], extras[0]]), top)
    direct_top[2], extra_top = early_top[:cut], early_top[cut:]
    for k in (0, *range(3, shares)):
        direct[k], extras[k] = direct[k][:cut], direct[k][cut:]
        if k:
            direct_top[k] = swap(direct[k], top)

    def spread(x):
        held, bit = {0: x}, top // 2
        while bit:
            for j in sorted(held):
                held[j ^ bit] = swap(held[j], bit)
            bit //= 2
        return [held[j] for j in sorted(held)]

    metas = spread(jnp.stack([x[:, :token_count] for x in (extras[0], extra_top)]))
    metas = jnp.concatenate([jnp.stack([m[b] for m in metas]) for b in range(2)], 0)
    metas = metas.astype(jnp.float32).reshape(experts, micros, 8, token_count)
    gap = metas[:, :, 2] + metas[:, :, 3] + metas[:, :, 4]
    weight_first, weight_second = jax.nn.sigmoid(gap), jax.nn.sigmoid(-gap)
    meta = jnp.stack(
        [
            metas[:, :, 0],
            metas[:, :, 1],
            weight_first,
            weight_second,
        ],
        2,
    ).reshape(experts, 4 * micros, token_count)

    places, weights, kept = find_places(meta, cap)
    last = join([direct[1]], [places])
    direct[1], extras[1] = last[:cut], last[cut:]
    direct_top[1] = swap(direct[1], top)

    def gather(which, gates):
        pieces = []
        for k in range(which * together, (which + 1) * together):
            pieces.append(spread(join([direct[k], direct_top[k], pairs[k]], gates)))
        tokens = pieces[0]
        if together > 1:
            order = jnp.arange(together) ^ (mine % together)
            tokens = []
            for j in range(top):
                stacked = jnp.take(jnp.stack([piece[j] for piece in pieces]), order, axis=0)
                tokens.append(stacked.transpose(1, 0, 2).reshape(-1, together * share))
        return tokens

    fetch_gates = [[], [pairs[2]]]
    held = []
    for i in range(half):
        gates = fetch_gates[i] if i < len(fetch_gates) else []
        held.append(fetch(sets[i], down_weights, together * share, gates))
    gates = []
    if together == 1:
        one, three = sets[half:]
        ahead = spread(join([direct[one], pairs[one], direct[three]]))
        gates = []
    rows = [fill_rows(places, weights, gather(which, []), cut, gates) for which in sets[:half]]
    total, done, held = multiply_first(sets[half:], rows, held, down_weights)
    extras[2] = join([near], [done])
    scores = 0.0
    for k in range(shares):
        terms = extras[k][:, :token_count].astype(jnp.float32).reshape(micros, 8, token_count)
        scores += terms[:, 5] + terms[:, 6] + terms[:, 7]
    slope = jnp.where(kept > 0, weight_first[0] * weight_second[0] * scores, 0.0)
    moved_logits = jnp.stack([slope, -slope], -1).astype(jnp.bfloat16)[None]

    if together > 1:
        tokens = [gather(which, [done]) for which in sets[half:]]
        spots = [((i, 0), (i, cut), (i, 2 * cut)) for i in range(len(tokens))]
    else:
        rest = join([direct_top[one], direct_top[three], pairs[three]], [done])
        tokens, both = [ahead, spread(rest)], 2 * (micros * token_count - cut)
        spots = [((0, 0), (1, 0), (0, cut)), ((0, cut + both), (1, cut), (1, 2 * cut))]
    hidden = multiply_last(places, weights, tokens, spots, held, total, experts, cut)
    return hidden.transpose(0, 1, 2, 4, 3, 5), moved_logits


def solution(mesh):
    in_specs = (
        P("pipe", None, "expert", "dp"),
        P("pipe", None, "expert", None, "dp"),
        P("pipe", None, "expert", None),
        P("pipe", None, "expert", None),
        P("expert", "dp", None),
    )
    out_specs = (P("pipe", None, "expert", None, None, "dp"), P("pipe", None, "expert", None))
    return jax.shard_map(
        per_device, mesh=mesh, in_specs=in_specs, out_specs=out_specs, check_vma=False
    )
```
